32 devices in a mesh: row: 4 (over z), col: 8 (over y, x, core).
Axes of the slice: x: 2, y: 2, z: 4, core: 2. Of those that a mesh axis runs over, the one named last changes fastest.
Arguments:
- feature: bfloat16 [64, 32, 1024], P(None, 'row', 'col'), may hold values from -6 to 6
- cotangent: bfloat16 [64, 32, 1024], P(None, 'row', 'col'), may hold values from -6 to 6
- order_weight: bfloat16 [6, 64, 64], replicated, may hold values from -0.75 to 0.75
- pixel_mask: int32 [32, 1024], P('row', 'col'), may hold values 0 or 1
Outputs:
- grad_feature: bfloat16 [64, 32, 1024], P(None, 'row', 'col')
- grad_order: float32 [6, 64, 64], replicated
The draws below stay inside these ranges and needn't reach their ends.
Inputs may be any that keep to these rules, and one draw needn't show every extreme that they name: `pixel_mask`: 1 where a pixel is observed, 0 where it is masked.
All inputs are finite; a program needn't handle non-finite values. No bound on the sum of `pixel_mask` on one device may be relied on, other than what follows from the above.
Results may differ from the reference program's by a relative error of at most 0.0054.
Values may be sent and summed in bfloat16 or wider, within the bound.
No kernel may reach another device: no remote copies, remote signals or barrier semaphores. Data moves between devices by JAX's collectives and lax.ppermute only.
A program may use at most 64 MiB of HBM per device.

```python
import math
import jax
import jax.numpy as jnp
from jax import lax

C = 64
K = 6
NH = 32
NW = 1024


def plant(values, stream_key, low, high):
    shape = values.shape
    place = [jax.random.randint(jax.random.fold_in(stream_key, axis), (), 0, shape[axis]) for axis in range(len(shape))]
    values = values.at[tuple(place)].set(low)
    longest = shape.index(max(shape))
    place[longest] = (place[longest] + 1) % shape[longest]
    return values.at[tuple(place)].set(high)


def level_of(stream_key, shape, cuts, low, top_value):
    factor_of = 1.0
    for axis_at, parts in cuts:
        draws = jax.random.uniform(jax.random.fold_in(jax.random.fold_in(stream_key, 6), axis_at), (parts,), jnp.float32, low / len(cuts), top_value / len(cuts))
        factor_of = factor_of * jnp.repeat(jnp.exp(draws), shape[axis_at] // parts).reshape((-1,) + (1,) * (len(shape) - 1 - axis_at))
    return factor_of


def scatter_about(stream_key, shape, deviation, most, shards=(), kind=jnp.bfloat16):
    level = level_of(stream_key, shape, shards, -0.22, 0.18) if shards else 1.0
    drawn = jax.random.normal(stream_key, shape, jnp.float32) * deviation * level
    return jnp.minimum(jnp.maximum(drawn, -most), most).astype(kind)


def setup_inputs(seed: int = 0) -> dict:
    splits = jax.random.split(jax.random.key(seed), 5)
    return {
        "feature": scatter_about(splits[0], (C, NH, NW), 1.0, 6.0, ((1, 4), (2, 8))),
        "cotangent": scatter_about(splits[1], (C, NH, NW), 1.0, 6.0, ((1, 4), (2, 8))),
        "order_weight": scatter_about(splits[2], (K, C, C), C ** -0.5, 0.75),
        "pixel_mask": plant((jax.random.randint(splits[3], (NH, NW), 0, 10) < 9).astype(jnp.int32), jax.random.fold_in(splits[3], 1), 0, 1),
    }


channel_block = 8

def neighbour_sum(u):
    row_sums = u[..., :-2, :] + u[..., 1:-1, :] + u[..., 2:, :]
    box = row_sums[..., :-2] + row_sums[..., 1:-1] + row_sums[..., 2:]
    return box - u[..., 1:-1, 1:-1]

def pad_rim(u):
    return jnp.pad(u, [(0, 0)] * (u.ndim - 2) + [(1, 1), (1, 1)])

def reference(feature, cotangent, order_weight, pixel_mask):
    mask_float = pixel_mask.astype(jnp.float32)
    degree = mask_float * neighbour_sum(pad_rim(mask_float))
    scales = mask_float / jnp.sqrt(jnp.maximum(degree, 1.0))

    def laplacian(v):
        return -scales * neighbour_sum(pad_rim(scales * v.astype(jnp.float32)))
    cot_flat = cotangent.reshape(C, NH * NW)

    def one_block(offset):
        feat_block = lax.dynamic_slice_in_dim(feature, offset, channel_block, 0)
        weight_block = lax.dynamic_slice_in_dim(order_weight, offset, channel_block, 1)

        def mix(k):
            return jnp.dot(weight_block[k], cot_flat, preferred_element_type=jnp.float32).reshape(channel_block, NH, NW)

        def order_grad(term):
            return lax.dot_general(term.reshape(channel_block, NH * NW), cot_flat, (((1,), (1,)), ((), ())), preferred_element_type=jnp.float32)
        cheb_terms = [feat_block, laplacian(feat_block).astype(jnp.bfloat16)]
        for k in range(2, K):
            cheb_terms.append((2.0 * laplacian(cheb_terms[k - 1]) - cheb_terms[k - 2].astype(jnp.float32)).astype(jnp.bfloat16))
        grads = jnp.stack([order_grad(t) for t in cheb_terms])
        adj_next = mix(K - 1).astype(jnp.bfloat16)
        adj_after = None
        for k in range(K - 2, 0, -1):
            update = mix(k) + 2.0 * laplacian(adj_next)
            if adj_after is not None:
                update = update - adj_after.astype(jnp.float32)
            adj_after, adj_next = (adj_next, update.astype(jnp.bfloat16))
        grad_block = (mix(0) + laplacian(adj_next) - adj_after.astype(jnp.float32)).astype(jnp.bfloat16)
        return (grad_block, grads)
    offsets = jnp.arange(0, C, channel_block, dtype=jnp.int32)
    blocks, grads = lax.map(one_block, offsets)
    grad_feature = blocks.reshape(C, NH, NW)
    grad_order = jnp.transpose(grads, (1, 0, 2, 3)).reshape(K, C, C) / math.sqrt(NH * NW)
    return (grad_feature, grad_order)
```

```python
import functools
import math

import jax
import jax.numpy as jnp
from jax import lax
from jax.experimental import pallas as pl
from jax.experimental.pallas import tpu as pltpu
from jax.sharding import PartitionSpec as P

RIM = 8
F32 = jnp.float32
BF16 = jnp.bfloat16
NT = (((1,), (1,)), ((), ()))


def iota(shape, dim):
    return lax.broadcasted_iota(jnp.int32, shape, dim)


def swap_halves(x):
    return pltpu.roll(x, x.shape[-1] // 2, x.ndim - 1)


def even_place(axis):
    return lax.axis_index(axis) % 2 == 0


def even_parity():
    place = lax.axis_index("row") * lax.axis_size("col") + lax.axis_index("col")
    for shift in (16, 8, 4, 2, 1):
        place = place ^ (place >> shift)
    return place % 2 == 0


def in_order(axis, first, second):
    even, place = even_place(axis), lax.axis_index(axis)
    before, after = jnp.where(even, second, first), jnp.where(even, first, second)
    return jnp.where(place == 0, 0.0, before), jnp.where(place == lax.axis_size(axis) - 1, 0.0, after)


def mask_kernel(mask_ref, out_ref):
    mask = mask_ref[...].astype(F32)
    out_ref[...] = jnp.concatenate([mask, jnp.zeros_like(mask)], axis=0).astype(BF16)


def pack_kernel(halo, cot_ref, mask_ref, body_ref, first_ref, second_ref, wide_ref):
    channels, rows, cols = cot_ref.shape
    half, lanes = cols // 2, 2 * channels
    wide_ref[...] = cot_ref[...].astype(F32).reshape(channels * rows, cols)
    fold = (iota((half, cols), 1) % half == iota((half, cols), 0)).astype(BF16)
    left = iota((channels, cols), 1) < half
    stacked = []
    for r in range(rows):
        row = wide_ref[pl.ds(r, channels, stride=rows), :]
        stacked += [jnp.where(left, row, 0.0), jnp.where(left, 0.0, row)]
    stacked = jnp.concatenate(stacked, axis=0).astype(BF16)
    body = lax.dot_general(fold, stacked, NT, preferred_element_type=F32)
    for r in range(rows):
        body_ref[r * half : (r + 1) * half, :] = body[:, r * lanes : (r + 1) * lanes].astype(BF16)
    south, count = even_place("row"), halo * half
    for out_ref, lower in ((first_ref, south), (second_ref, jnp.logical_not(south))):
        start = pl.multiple_of(jnp.where(lower, rows * half - count, 0), half)
        out_ref[:count, :] = body_ref[pl.ds(start, count), :]
        out_ref[count:, :] = mask_ref[...]


def early_kernel(feature_ref, weight_ref, feature_out_ref, rim_out_ref, weight_out_ref, wide_ref):
    channels, rows, cols = feature_ref.shape
    lanes = 2 * channels
    wide_ref[...] = feature_ref[...].astype(F32).reshape(channels * rows, cols)
    left = iota((channels, cols), 1) < cols // 2
    for q in range(rows // 2):
        even = wide_ref[pl.ds(2 * q, channels, stride=rows), :]
        odd = wide_ref[pl.ds(2 * q + 1, channels, stride=rows), :]
        at = slice(q * cols, (q + 1) * cols)
        feature_out_ref[:channels, at] = jnp.where(left, even, swap_halves(odd)).astype(BF16)
        feature_out_ref[channels:, at] = jnp.where(left, swap_halves(even), odd).astype(BF16)
    half, shape = cols // 2, (rows * cols // 2, rows * RIM)
    pixel, target = iota(shape, 0), iota(shape, 1)
    here = target // RIM * half + target % RIM
    sides = [
        jnp.dot(feature_out_ref[...], (pixel == here + skip).astype(BF16), preferred_element_type=F32)
        for skip in (0, half - RIM)
    ]
    rim_out_ref[:channels, :] = sides[0][:channels].astype(BF16)
    rim_out_ref[channels:, :] = sides[1][channels:].astype(BF16)
    for k in range(weight_ref.shape[0]):
        weight = weight_ref[k].astype(F32) * (-1.0) ** k
        blank = jnp.zeros_like(weight)
        at = slice(k * lanes, (k + 1) * lanes)
        weight_out_ref[:channels, at] = jnp.concatenate([weight, blank], axis=1).astype(BF16)
        weight_out_ref[channels:, at] = jnp.concatenate([blank, weight], axis=1).astype(BF16)


def row_pieces(halo, half, body_ref, first_ref, second_ref, begin, size):
    rows = body_ref.shape[0] // half

    def piece(ref, r):
        return ref[r * half + begin : r * half + begin + size, :].astype(F32)

    received = [in_order("row", piece(first_ref, r), piece(second_ref, r)) for r in range(halo)]
    return [north for north, _ in received] + [piece(body_ref, r) for r in range(rows)] + [south for _, south in received]


def all_masks(halo, half, mask_ref, first_ref, second_ref):
    rows, begin = mask_ref.shape[0] // 2, halo * half
    north, south = in_order("row", first_ref[begin:, :].astype(F32), second_ref[begin:, :].astype(F32))
    return jnp.concatenate([north[:rows], mask_ref[...].astype(F32)[:rows], south[:rows]], axis=0)


def strips_kernel(halo, body_ref, mask_ref, second_ref, first_ref, to_first_ref, to_second_ref):
    rows = mask_ref.shape[0] // 2
    half = body_ref.shape[0] // rows
    total = rows + 2 * halo
    marks = 3 * rows
    masks = all_masks(halo, half, mask_ref, first_ref, second_ref)
    leading = row_pieces(halo, half, body_ref, first_ref, second_ref, 0, 2 * RIM)
    trailing = row_pieces(halo, half, body_ref, first_ref, second_ref, half - 2 * RIM, 2 * RIM)
    low = iota((RIM, body_ref.shape[1]), 1) < body_ref.shape[1] // 2
    west, east = [], []
    for n in range(total // 2):
        west.append(jnp.where(low, leading[n][:RIM], swap_halves(leading[n + total // 2][:RIM])))
        east.append(jnp.where(low, swap_halves(trailing[n][RIM:]), trailing[n + total // 2][RIM:]))
    spare = to_first_ref.shape[0] - total // 2 * RIM - marks
    blank = [jnp.zeros((spare, body_ref.shape[1]), F32)] if spare else []
    west, east = (jnp.concatenate([masks, *x] + blank, axis=0) for x in (west, east))
    even = even_place("col")
    to_first_ref[...] = jnp.where(even, east, west).astype(BF16)
    to_second_ref[...] = jnp.where(even, west, east).astype(BF16)


def compact_scales(mask):
    rows, cols = mask.shape
    column = mask + pltpu.roll(mask, 1, 0) + pltpu.roll(mask, rows - 1, 0)
    degree = mask * (column + pltpu.roll(column, 1, 1) + pltpu.roll(column, cols - 1, 1) - mask)
    return jnp.transpose(mask * jnp.sqrt(2.0 / jnp.maximum(degree, 1.0)), (1, 0))


def spread_scales(left, right, scale_ref):
    (tall, marks), lanes = left.shape, scale_ref.shape[1]
    total = scale_ref.shape[0] // tall
    spare = jnp.zeros((tall, lanes // 2 - marks), F32)
    both = jnp.concatenate([left, spare, right, spare], axis=1)
    lane = iota((tall, lanes), 1)
    start = jnp.where(lane < lanes // 2, 0, lanes // 2) + (marks - total) // 2
    for q in range(total):
        picked = jnp.take_along_axis(both, start + q, axis=1, mode="promise_in_bounds")
        scale_ref[q * tall : (q + 1) * tall, :] = picked


def next_term(k, tall, scale_ref, newer_ref, older_ref, visit):
    total = scale_ref.shape[0] // tall

    def at(q):
        return slice(q * tall, (q + 1) * tall)

    def weighted(q):
        return scale_ref[at(q), :] * newer_ref[at(q), :]

    above, here = weighted(k - 1), weighted(k)
    for q in range(k, total - k):
        below = weighted(q + 1)
        column = above + here + below
        nearby = column + pltpu.roll(column, 1, 0) + pltpu.roll(column, tall - 1, 0) - here
        fresh = scale_ref[at(q), :] * nearby
        fresh = 0.5 * fresh if k == 1 else fresh - older_ref[at(q), :]
        older_ref[at(q), :] = fresh
        visit(q, fresh)
        above, here = here, below


def order_products(b, lanes, feature, terms):
    channels = lanes // 2
    product = jnp.dot(feature, terms[:, 2 * b * lanes : 2 * (b + 1) * lanes], preferred_element_type=F32)
    near, far = product[:channels], product[channels:]
    even = near[:, :lanes] + swap_halves(far[:, :lanes])
    odd = swap_halves(near[:, lanes:]) + far[:, lanes:]
    return jnp.where(iota((channels, lanes), 1) < channels, even, -odd)


def interior_kernel(
    orders, body_ref, mask_ref, second_ref, first_ref, feature_ref, terms_ref, sums_ref, own_ref, even_ref, odd_ref, scale_ref
):
    rows, cols = mask_ref.shape[0] // 2, mask_ref.shape[1]
    half, halo, lanes = cols // 2, orders - 1, body_ref.shape[1]
    tall = half + 2 * RIM
    across = compact_scales(all_masks(halo, half, mask_ref, first_ref, second_ref))
    rim = jnp.zeros((RIM, across.shape[1]), F32)
    left = jnp.concatenate([rim, across[: half + RIM]], axis=0)
    right = jnp.concatenate([across[half - RIM :], rim], axis=0)
    spread_scales(left, right, scale_ref)
    low = iota((RIM, lanes), 1) < lanes // 2
    for q, middle in enumerate(row_pieces(halo, half, body_ref, first_ref, second_ref, 0, half)):
        at = q * tall
        odd_ref[at : at + RIM, :] = jnp.where(low, 0.0, swap_halves(middle[half - RIM :]))
        odd_ref[at + RIM : at + RIM + half, :] = middle
        odd_ref[at + RIM + half : at + tall, :] = jnp.where(low, swap_halves(middle[:RIM]), 0.0)
        at = q * 3 * RIM
        tail = half - 2 * RIM
        own_ref[at : at + RIM, :] = jnp.where(low, 0.0, middle[tail : tail + RIM])
        own_ref[at + RIM : at + 2 * RIM, :] = jnp.where(low, middle[:RIM], middle[tail + RIM :])
        own_ref[at + 2 * RIM : at + 3 * RIM, :] = jnp.where(low, middle[RIM : 2 * RIM], 0.0)
    terms_ref[:, :lanes] = body_ref[...]
    newer, older = odd_ref, even_ref
    for k in range(1, orders):
        def keep(q, fresh):
            r = q - halo
            if 0 <= r < rows:
                columns = slice(k * lanes, (k + 1) * lanes)
                first = jnp.where(low, 0.0, fresh[RIM : 2 * RIM])
                last = jnp.where(low, fresh[half : half + RIM], 0.0)
                kept = jnp.concatenate([first, fresh[2 * RIM : half], last], axis=0)
                terms_ref[r * half : (r + 1) * half, columns] = kept.astype(BF16)

        next_term(k, tall, scale_ref, newer, older, keep)
        newer, older = older, newer
        if k % 2:
            sums_ref[k // 2] = order_products(k // 2, lanes, feature_ref[...], terms_ref)


def edge_kernel(
    orders, own_ref, mask_ref, north_second_ref, north_first_ref, second_ref, first_ref, rim_ref, sums_ref,
    terms_ref, keep_ref, give_ref, even_ref, odd_ref, scale_ref, wide_ref,
):
    rows, cols = mask_ref.shape[0] // 2, mask_ref.shape[1]
    half, halo, lanes = cols // 2, orders - 1, own_ref.shape[1]
    channels, total, tall = lanes // 2, rows + 2 * halo, 3 * RIM
    west, east = in_order("col", first_ref[...].astype(F32), second_ref[...].astype(F32))
    lower = iota((3 * rows, cols), 1) < half
    centre = all_masks(halo, half, mask_ref, north_first_ref, north_second_ref)
    beside = jnp.where(lower, east[: 3 * rows], west[: 3 * rows])
    across = compact_scales(jnp.concatenate([centre, beside], axis=1))
    left = jnp.concatenate([across[2 * cols - RIM :], across[: 2 * RIM]], axis=0)
    spread_scales(left, across[cols - 2 * RIM : cols + RIM], scale_ref)

    low = iota((RIM, lanes), 1) < channels
    for q in range(total):
        n, upper_row = q % (total // 2), q >= total // 2
        strip = slice(3 * rows + n * RIM, 3 * rows + (n + 1) * RIM)
        before = swap_halves(west[strip]) if upper_row else west[strip]
        after = east[strip] if upper_row else swap_halves(east[strip])
        at = q * tall
        odd_ref[at : at + RIM, :] = jnp.where(low, before, own_ref[at : at + RIM, :])
        odd_ref[at + RIM : at + 2 * RIM, :] = own_ref[at + RIM : at + 2 * RIM, :]
        odd_ref[at + 2 * RIM : at + tall, :] = jnp.where(low, own_ref[at + 2 * RIM : at + tall, :], after)

    wide_ref[:, :lanes] = jnp.zeros((rows * RIM, lanes), F32)
    newer, older = odd_ref, even_ref
    for k in range(1, orders):
        def keep(q, fresh):
            r = q - halo
            if 0 <= r < rows:
                wide_ref[r * RIM : (r + 1) * RIM, k * lanes : (k + 1) * lanes] = fresh[RIM : 2 * RIM]

        next_term(k, tall, scale_ref, newer, older, keep)
        newer, older = older, newer
    terms_ref[...] = wide_ref[...].astype(BF16)
    upper = even_parity()
    for b in range(orders // 2):
        block = sums_ref[b] + order_products(b, lanes, rim_ref[...], terms_ref)
        a, b_half = block[: channels // 2], block[channels // 2 :]
        keep_ref[b] = jnp.where(upper, a, b_half)
        give_ref[b] = jnp.where(upper, b_half, a)


def mix_kernel(weight_ref, inner_ref, rim_ref, grad_ref, wide_ref, terms_ref):
    channels, rows, cols = grad_ref.shape
    half, lanes = cols // 2, 2 * channels
    terms_ref[...] = inner_ref[...]
    lane, sublane = iota((2 * RIM, lanes), 1), iota((2 * RIM, lanes), 0)
    first_columns = jnp.logical_and(lane < channels, sublane < RIM)
    last_columns = jnp.logical_and(lane >= channels, sublane >= RIM)
    for k in range(1, rim_ref.shape[1] // lanes):
        columns = slice(k * lanes, (k + 1) * lanes)
        rims = rim_ref[:, columns].astype(F32)
        for r in range(rows):
            twice = jnp.concatenate([rims[r * RIM : (r + 1) * RIM]] * 2, axis=0)
            for begin, chosen in ((r * half, first_columns), ((r + 1) * half - 2 * RIM, last_columns)):
                at = (slice(begin, begin + 2 * RIM), columns)
                terms_ref[at] = jnp.where(chosen, twice, inner_ref[at].astype(F32)).astype(BF16)
    low = iota((channels, cols), 1) < half
    mixed = lax.dot_general(weight_ref[...], terms_ref[...], NT, preferred_element_type=F32)
    for q in range(rows // 2):
        upper, lower = mixed[:channels, q * cols : (q + 1) * cols], mixed[channels:, q * cols : (q + 1) * cols]
        wide_ref[pl.ds(2 * q, channels, stride=rows), :] = jnp.where(low, upper, swap_halves(lower))
        wide_ref[pl.ds(2 * q + 1, channels, stride=rows), :] = jnp.where(low, swap_halves(upper), lower)
    grad_ref[...] = wide_ref[...].reshape(channels, rows, cols).astype(BF16)


def finish_kernel(divisor, mine_ref, other_ref, out_ref):
    orders, channels, _ = out_ref.shape
    upper = even_parity()
    for b in range(orders // 2):
        mine, other = mine_ref[b] / divisor, other_ref[b] / divisor
        block = jnp.concatenate([jnp.where(upper, mine, other), jnp.where(upper, other, mine)], axis=0)
        out_ref[2 * b] = block[:, :channels]
        out_ref[2 * b + 1] = block[:, channels:]


def call(kernel, outs, scratch, cost, *args):
    return pl.pallas_call(
        kernel,
        out_shape=outs,
        in_specs=[pl.BlockSpec(memory_space=pltpu.VMEM)] * len(args),
        out_specs=jax.tree.map(lambda _: pl.BlockSpec(memory_space=pltpu.VMEM), outs),
        scratch_shapes=scratch,
        compiler_params=pltpu.CompilerParams(vmem_limit_bytes=32 * 1024 * 1024),
        cost_estimate=pl.CostEstimate(flops=cost, bytes_accessed=1 << 20, transcendentals=0),
    )(*args)


def swap(x, partner):
    places = range(lax.axis_size("row") * lax.axis_size("col"))
    return lax.ppermute(x, ("row", "col"), [(i, partner(i)) for i in places])


def exchange_cols(first, second):
    across = lax.axis_size("col")

    def after_odd(i):
        row, col = i // across, i % across
        return row * across + (((col - 1) % across ^ 1) + 1) % across

    second = swap(second, after_odd)
    return swap(first, lambda i: i ^ 1), second


def exchange_rows(first, second):
    across, down = lax.axis_size("col"), lax.axis_size("row")

    def after_odd(i):
        row, col = i // across, i % across
        return i ^ 1 if row in (0, down - 1) else (((row - 1) ^ 1) + 1) * across + col

    return swap(first, lambda i: (i // across ^ 1) * across + i % across), swap(second, after_odd)


def sum_everywhere(keep, give, work, *args):
    across, down = lax.axis_size("col"), lax.axis_size("row")
    beside = list(range(1, across.bit_length() - 1))
    below = list(range(across.bit_length() - 1, (across * down).bit_length() - 1))
    turns = [(beside[n : n + 1], below[n : n + 1]) for n in range(max(len(beside), len(below)))]
    even = [bit for a, b in turns for bit in a + b]
    odd = [bit for a, b in turns for bit in b + a]
    mine = keep + swap(give, lambda i: i ^ 1)
    for n, bits in enumerate(zip(even, odd)):
        received = swap(mine, lambda i: i ^ (1 << bits[i.bit_count() % 2]) ^ 1)
        if n == 0:
            _, *args = lax.optimization_barrier((mine, *args))
            received, done = lax.optimization_barrier((received, work(*args)))
        mine = mine + received
    return mine, swap(mine, lambda i: i ^ 1), done


def body(feature, cotangent, order_weight, pixel_mask):
    orders, channels, _ = order_weight.shape
    _, rows, cols = feature.shape
    half, lanes, halo = cols // 2, 2 * channels, orders - 1
    tall, total = half + 2 * RIM, rows + 2 * halo
    shape = jax.ShapeDtypeStruct
    wide = pltpu.VMEM((channels * rows, cols), F32)
    marks = shape((2 * rows, cols), BF16)

    mask16 = call(mask_kernel, marks, [], 1 << 31, pixel_mask)
    sent = shape((halo * half + 2 * rows, lanes), BF16)
    cot_body, first, second = call(
        functools.partial(pack_kernel, halo), [shape((rows * half, lanes), BF16), sent, sent], [wide], 1 << 20,
        cotangent, mask16,
    )
    first, second = exchange_rows(first, second)
    features, rims, weights = call(
        early_kernel,
        [shape((lanes, rows * half), BF16), shape((lanes, rows * RIM), BF16), shape((lanes, orders * lanes), BF16)],
        [wide], 1 << 20, feature, order_weight,
    )
    sent = shape((-(-(3 * rows + total // 2 * RIM) // 16) * 16, lanes), BF16)
    west_first, west_second = call(
        functools.partial(strips_kernel, halo), [sent, sent], [], 1 << 16, cot_body, mask16, second, first
    )
    west_first, west_second = exchange_cols(west_first, west_second)
    buffer = pltpu.VMEM((total * tall, lanes), F32)
    small = pltpu.VMEM((total * 3 * RIM, lanes), F32)
    terms = shape((rows * half, orders * lanes), BF16)
    rim_terms = shape((rows * RIM, orders * lanes), BF16)
    part = shape((orders // 2, channels // 2, lanes), F32)
    inner, sums, own = call(
        functools.partial(interior_kernel, orders),
        [terms, shape((orders // 2, channels, lanes), F32), shape((total * 3 * RIM, lanes), F32)],
        [buffer, buffer, buffer], 1 << 28, cot_body, mask16, second, first, features,
    )
    outer, keep, give = call(
        functools.partial(edge_kernel, orders), [rim_terms, part, part],
        [small, small, small, pltpu.VMEM(rim_terms.shape, F32)], 1 << 26,
        own, mask16, second, first, west_second, west_first, rims, sums,
    )
    mix = functools.partial(
        call, mix_kernel, shape((channels, rows, cols), BF16), [wide, pltpu.VMEM(terms.shape, BF16)], 1 << 20
    )
    mine, other, grad_feature = sum_everywhere(keep, give, mix, weights, inner, outer)
    pixel_count = rows * cols * lax.axis_size("row") * lax.axis_size("col")
    grad_order = call(
        functools.partial(finish_kernel, math.sqrt(pixel_count)),
        shape((orders, channels, channels), F32), [], 1 << 16, mine, other,
    )
    return (grad_feature, grad_order)


def solution(mesh):
    placed = (P(None, "row", "col"), P(None, "row", "col"), P(), P("row", "col"))
    return jax.shard_map(
        body, mesh=mesh, in_specs=placed, out_specs=(P(None, "row", "col"), P()), check_vma=False
    )
```

```python
import functools
import math

import jax
import jax.numpy as jnp
from jax import lax
from jax.experimental import pallas as pl
from jax.experimental.pallas import tpu as pltpu
from jax.sharding import PartitionSpec as P

RIM = 8
NOTES = 16
F32 = jnp.float32
BF16 = jnp.bfloat16
NT = (((1,), (1,)), ((), ()))


def iota(shape, dim):
    return lax.broadcasted_iota(jnp.int32, shape, dim)


def swap_halves(x):
    return pltpu.roll(x, x.shape[-1] // 2, x.ndim - 1)


def even_place(axis):
    return lax.axis_index(axis) % 2 == 0


def in_order(axis, first, second):
    even, place = even_place(axis), lax.axis_index(axis)
    before, after = jnp.where(even, second, first), jnp.where(even, first, second)
    return jnp.where(place == 0, 0.0, before), jnp.where(place == lax.axis_size(axis) - 1, 0.0, after)


def mask_kernel(mask_ref, out_ref):
    mask = mask_ref[...].astype(F32)
    out_ref[...] = jnp.concatenate([mask, jnp.zeros_like(mask)], axis=0).astype(BF16)


def pack_kernel(halo, cot_ref, mask_ref, body_ref, first_ref, second_ref, wide_ref):
    channels, rows, cols = cot_ref.shape
    half, lanes = cols // 2, 2 * channels
    wide_ref[...] = cot_ref[...].astype(F32).reshape(channels * rows, cols)
    fold = (iota((half, cols), 1) % half == iota((half, cols), 0)).astype(BF16)
    left = iota((channels, cols), 1) < half
    stacked = []
    for r in range(rows):
        row = wide_ref[pl.ds(r, channels, stride=rows), :]
        stacked += [jnp.where(left, row, 0.0), jnp.where(left, 0.0, row)]
    stacked = jnp.concatenate(stacked, axis=0).astype(BF16)
    body = lax.dot_general(fold, stacked, NT, preferred_element_type=F32)
    for r in range(rows):
        body_ref[r * half : (r + 1) * half, :] = body[:, r * lanes : (r + 1) * lanes].astype(BF16)
    south, count = even_place("row"), halo * half
    for out_ref, lower in ((first_ref, south), (second_ref, jnp.logical_not(south))):
        start = pl.multiple_of(jnp.where(lower, rows * half - count, 0), half)
        out_ref[:count, :] = body_ref[pl.ds(start, count), :]
        out_ref[count:, :] = mask_ref[...]


def early_kernel(feature_ref, weight_ref, feature_out_ref, rim_out_ref, weight_out_ref, wide_ref):
    channels, rows, cols = feature_ref.shape
    lanes = 2 * channels
    wide_ref[...] = feature_ref[...].astype(F32).reshape(channels * rows, cols)
    left = iota((channels, cols), 1) < cols // 2
    for q in range(rows // 2):
        even = wide_ref[pl.ds(2 * q, channels, stride=rows), :]
        odd = wide_ref[pl.ds(2 * q + 1, channels, stride=rows), :]
        at = slice(q * cols, (q + 1) * cols)
        feature_out_ref[:channels, at] = jnp.where(left, even, swap_halves(odd)).astype(BF16)
        feature_out_ref[channels:, at] = jnp.where(left, swap_halves(even), odd).astype(BF16)
    half, shape = cols // 2, (rows * cols // 2, rows * RIM)
    pixel, target = iota(shape, 0), iota(shape, 1)
    here = target // RIM * half + target % RIM
    sides = [
        jnp.dot(feature_out_ref[...], (pixel == here + skip).astype(BF16), preferred_element_type=F32)
        for skip in (0, half - RIM)
    ]
    rim_out_ref[:channels, :] = sides[0][:channels].astype(BF16)
    rim_out_ref[channels:, :] = sides[1][channels:].astype(BF16)
    for k in range(weight_ref.shape[0]):
        weight = weight_ref[k].astype(F32) * (-1.0) ** k
        blank = jnp.zeros_like(weight)
        at = slice(k * lanes, (k + 1) * lanes)
        weight_out_ref[:channels, at] = jnp.concatenate([weight, blank], axis=1).astype(BF16)
        weight_out_ref[channels:, at] = jnp.concatenate([blank, weight], axis=1).astype(BF16)


def row_pieces(halo, half, body_ref, first_ref, second_ref, begin, size):
    rows = body_ref.shape[0] // half

    def piece(ref, r):
        return ref[r * half + begin : r * half + begin + size, :].astype(F32)

    received = [in_order("row", piece(first_ref, r), piece(second_ref, r)) for r in range(halo)]
    return [north for north, _ in received] + [piece(body_ref, r) for r in range(rows)] + [south for _, south in received]


def all_masks(halo, half, mask_ref, first_ref, second_ref):
    rows, begin = mask_ref.shape[0] // 2, halo * half
    north, south = in_order("row", first_ref[begin:, :].astype(F32), second_ref[begin:, :].astype(F32))
    return jnp.concatenate([north[:rows], mask_ref[...].astype(F32)[:rows], south[:rows]], axis=0)


def edge_lanes(masks):
    cols = masks.shape[1]
    return pltpu.roll(masks, cols // 4, 1), pltpu.roll(masks, cols - cols // 4, 1)


def strips_kernel(halo, body_ref, mask_ref, second_ref, first_ref, to_first_ref, to_second_ref):
    rows = mask_ref.shape[0] // 2
    half = body_ref.shape[0] // rows
    total = rows + 2 * halo
    marks = 3 * rows
    masks = all_masks(halo, half, mask_ref, first_ref, second_ref)
    ahead, behind = edge_lanes(masks)
    leading = row_pieces(halo, half, body_ref, first_ref, second_ref, 0, 2 * RIM)
    trailing = row_pieces(halo, half, body_ref, first_ref, second_ref, half - 2 * RIM, 2 * RIM)
    low = iota((RIM, body_ref.shape[1]), 1) < body_ref.shape[1] // 2
    west, east = [], []
    for n in range(total // 2):
        west.append(jnp.where(low, leading[n][:RIM], swap_halves(leading[n + total // 2][:RIM])))
        east.append(jnp.where(low, swap_halves(trailing[n][RIM:]), trailing[n + total // 2][RIM:]))
    spare = to_first_ref.shape[0] - total // 2 * RIM - marks
    blank = [jnp.zeros((spare, body_ref.shape[1]), F32)] if spare else []
    west, east = (jnp.concatenate([marks_sent, *x] + blank, axis=0) for marks_sent, x in ((behind, west), (ahead, east)))
    even = even_place("col")
    to_first_ref[...] = jnp.where(even, east, west).astype(BF16)
    to_second_ref[...] = jnp.where(even, west, east).astype(BF16)


def compact_scales(mask):
    rows, cols = mask.shape
    column = mask + pltpu.roll(mask, 1, 0) + pltpu.roll(mask, rows - 1, 0)
    degree = mask * (column + pltpu.roll(column, 1, 1) + pltpu.roll(column, cols - 1, 1) - mask)
    return jnp.transpose(mask * jnp.sqrt(2.0 / jnp.maximum(degree, 1.0)), (1, 0))


def spread_scales(left, right, scale_ref):
    (tall, marks), lanes = left.shape, scale_ref.shape[1]
    total = scale_ref.shape[0] // tall
    spare = jnp.zeros((tall, lanes // 2 - marks), F32)
    both = jnp.concatenate([left, spare, right, spare], axis=1)
    lane = iota((tall, lanes), 1)
    start = jnp.where(lane < lanes // 2, 0, lanes // 2) + (marks - total) // 2
    for q in range(total):
        picked = jnp.take_along_axis(both, start + q, axis=1, mode="promise_in_bounds")
        scale_ref[q * tall : (q + 1) * tall, :] = picked


def next_term(k, tall, scale_ref, newer_ref, older_ref, visit):
    total = scale_ref.shape[0] // tall

    def at(q):
        return slice(q * tall, (q + 1) * tall)

    def weighted(q):
        return scale_ref[at(q), :] * newer_ref[at(q), :]

    above, here = weighted(k - 1), weighted(k)
    for q in range(k, total - k):
        below = weighted(q + 1)
        column = above + here + below
        nearby = column + pltpu.roll(column, 1, 0) + pltpu.roll(column, tall - 1, 0) - here
        fresh = scale_ref[at(q), :] * nearby
        fresh = 0.5 * fresh if k == 1 else fresh - older_ref[at(q), :]
        older_ref[at(q), :] = fresh
        visit(q, fresh)
        above, here = here, below


def order_products(b, lanes, feature, terms):
    channels = lanes // 2
    product = jnp.dot(feature, terms[:, 2 * b * lanes : 2 * (b + 1) * lanes], preferred_element_type=F32)
    near, far = product[:channels], product[channels:]
    even = near[:, :lanes] + swap_halves(far[:, :lanes])
    odd = swap_halves(near[:, lanes:]) + far[:, lanes:]
    return jnp.where(iota((channels, lanes), 1) < channels, even, -odd)


def interior_kernel(
    orders, body_ref, mask_ref, second_ref, first_ref, feature_ref, terms_ref, sums_ref, own_ref, centre_ref, even_ref, odd_ref, scale_ref
):
    rows, cols = mask_ref.shape[0] // 2, mask_ref.shape[1]
    half, halo, lanes = cols // 2, orders - 1, body_ref.shape[1]
    tall = half + 2 * RIM
    masks = all_masks(halo, half, mask_ref, first_ref, second_ref)
    ahead, behind = edge_lanes(masks)
    centre_ref[...] = jnp.where(iota(masks.shape, 1) < half, ahead, behind)
    across = compact_scales(masks)
    rim = jnp.zeros((RIM, across.shape[1]), F32)
    left = jnp.concatenate([rim, across[: half + RIM]], axis=0)
    right = jnp.concatenate([across[half - RIM :], rim], axis=0)
    spread_scales(left, right, scale_ref)
    low = iota((RIM, lanes), 1) < lanes // 2
    for q, middle in enumerate(row_pieces(halo, half, body_ref, first_ref, second_ref, 0, half)):
        at = q * tall
        odd_ref[at : at + RIM, :] = jnp.where(low, 0.0, swap_halves(middle[half - RIM :]))
        odd_ref[at + RIM : at + RIM + half, :] = middle
        odd_ref[at + RIM + half : at + tall, :] = jnp.where(low, swap_halves(middle[:RIM]), 0.0)
        at = q * 3 * RIM
        tail = half - 2 * RIM
        own_ref[at : at + RIM, :] = jnp.where(low, 0.0, middle[tail : tail + RIM])
        own_ref[at + RIM : at + 2 * RIM, :] = jnp.where(low, middle[:RIM], middle[tail + RIM :])
        own_ref[at + 2 * RIM : at + 3 * RIM, :] = jnp.where(low, middle[RIM : 2 * RIM], 0.0)
    terms_ref[:, :lanes] = body_ref[...]
    newer, older = odd_ref, even_ref
    for k in range(1, orders):
        def keep(q, fresh):
            r = q - halo
            if 0 <= r < rows:
                columns = slice(k * lanes, (k + 1) * lanes)
                first = jnp.where(low, 0.0, fresh[RIM : 2 * RIM])
                last = jnp.where(low, fresh[half : half + RIM], 0.0)
                kept = jnp.concatenate([first, fresh[2 * RIM : half], last], axis=0)
                terms_ref[r * half : (r + 1) * half, columns] = kept.astype(BF16)

        next_term(k, tall, scale_ref, newer, older, keep)
        newer, older = older, newer
        if k % 2:
            sums_ref[k // 2] = order_products(k // 2, lanes, feature_ref[...], terms_ref)


def store_sums(message_ref, blocks, exponent):
    scale, at = jnp.exp2(9.0 - exponent), 0
    for block in blocks:
        for row in range(0, block.shape[0], 8):
            message_ref[at : at + 8, :] = block[row : row + 8] * scale
            at += 8
    message_ref[at:, :] = jnp.concatenate([exponent] * (NOTES // 8), axis=0)


def add_kernel(mine_ref, received_ref, out_ref):
    notes = mine_ref.shape[0] - NOTES
    mine, received = mine_ref[notes : notes + 8, :], received_ref[notes : notes + 8, :]
    scales = jnp.exp2(mine - 9.0), jnp.exp2(received - 9.0)
    sums = []
    for row in range(0, notes, 8):
        at = slice(row, row + 8)
        sums.append(mine_ref[at, :] * scales[0] + received_ref[at, :] * scales[1])
    if out_ref.shape[0] == notes:
        out_ref[...] = jnp.concatenate(sums, axis=0)
    else:
        store_sums(out_ref, sums, jnp.maximum(mine, received) + 1.0)


def edge_kernel(
    orders, own_ref, centre_ref, second_ref, first_ref, rim_ref, sums_ref,
    terms_ref, message_ref, even_ref, odd_ref, scale_ref, wide_ref,
):
    rows, cols = centre_ref.shape[0] // 3, centre_ref.shape[1]
    halo, lanes, quarter = orders - 1, own_ref.shape[1], cols // 4
    channels, total, tall = lanes // 2, rows + 2 * halo, 3 * RIM
    west, east = in_order("col", first_ref[...].astype(F32), second_ref[...].astype(F32))
    lane = iota((3 * rows, cols), 1)
    masks = jnp.where(lane < quarter, west[: 3 * rows], jnp.where(lane < 3 * quarter, centre_ref[...], east[: 3 * rows]))
    across = compact_scales(masks)
    begin = quarter - RIM
    spread_scales(across[begin : begin + tall], across[3 * quarter - 2 * RIM : 3 * quarter + RIM], scale_ref)

    low = iota((RIM, lanes), 1) < channels
    for q in range(total):
        n, upper_row = q % (total // 2), q >= total // 2
        strip = slice(3 * rows + n * RIM, 3 * rows + (n + 1) * RIM)
        before = swap_halves(west[strip]) if upper_row else west[strip]
        after = east[strip] if upper_row else swap_halves(east[strip])
        at = q * tall
        odd_ref[at : at + RIM, :] = jnp.where(low, before, own_ref[at : at + RIM, :])
        odd_ref[at + RIM : at + 2 * RIM, :] = own_ref[at + RIM : at + 2 * RIM, :]
        odd_ref[at + 2 * RIM : at + tall, :] = jnp.where(low, own_ref[at + 2 * RIM : at + tall, :], after)

    wide_ref[:, :lanes] = jnp.zeros((rows * RIM, lanes), F32)
    newer, older = odd_ref, even_ref
    for k in range(1, orders):
        def keep(q, fresh):
            r = q - halo
            if 0 <= r < rows:
                wide_ref[r * RIM : (r + 1) * RIM, k * lanes : (k + 1) * lanes] = fresh[RIM : 2 * RIM]

        next_term(k, tall, scale_ref, newer, older, keep)
        newer, older = older, newer
    terms_ref[...] = wide_ref[...].astype(BF16)
    blocks = [sums_ref[b] + order_products(b, lanes, rim_ref[...], terms_ref) for b in range(orders // 2)]
    tiles = [jnp.abs(block[row : row + 8]) for block in blocks for row in range(0, channels, 8)]
    largest = functools.reduce(jnp.maximum, tiles)
    exponent = jnp.floor(jnp.log2(jnp.maximum(largest, 1e-30))) + 1.0
    store_sums(message_ref, blocks, exponent)


def mix_kernel(weight_ref, inner_ref, rim_ref, grad_ref, wide_ref, terms_ref):
    channels, rows, cols = grad_ref.shape
    half, lanes = cols // 2, 2 * channels
    terms_ref[...] = inner_ref[...]
    lane, sublane = iota((2 * RIM, lanes), 1), iota((2 * RIM, lanes), 0)
    first_columns = jnp.logical_and(lane < channels, sublane < RIM)
    last_columns = jnp.logical_and(lane >= channels, sublane >= RIM)
    for k in range(1, rim_ref.shape[1] // lanes):
        columns = slice(k * lanes, (k + 1) * lanes)
        rims = rim_ref[:, columns].astype(F32)
        for r in range(rows):
            twice = jnp.concatenate([rims[r * RIM : (r + 1) * RIM]] * 2, axis=0)
            for begin, chosen in ((r * half, first_columns), ((r + 1) * half - 2 * RIM, last_columns)):
                at = (slice(begin, begin + 2 * RIM), columns)
                terms_ref[at] = jnp.where(chosen, twice, inner_ref[at].astype(F32)).astype(BF16)
    low = iota((channels, cols), 1) < half
    mixed = lax.dot_general(weight_ref[...], terms_ref[...], NT, preferred_element_type=F32)
    for q in range(rows // 2):
        upper, lower = mixed[:channels, q * cols : (q + 1) * cols], mixed[channels:, q * cols : (q + 1) * cols]
        wide_ref[pl.ds(2 * q, channels, stride=rows), :] = jnp.where(low, upper, swap_halves(lower))
        wide_ref[pl.ds(2 * q + 1, channels, stride=rows), :] = jnp.where(low, swap_halves(upper), lower)
    grad_ref[...] = wide_ref[...].reshape(channels, rows, cols).astype(BF16)


def finish_kernel(divisor, mine_ref, other_ref, out_ref):
    channels = out_ref.shape[1]
    for b in range(out_ref.shape[0] // 2):
        at = slice(b * channels, (b + 1) * channels)
        block = (mine_ref[at, :] + other_ref[at, :]) / divisor
        out_ref[2 * b] = block[:, :channels]
        out_ref[2 * b + 1] = block[:, channels:]


def call(kernel, outs, scratch, cost, *args):
    return pl.pallas_call(
        kernel,
        out_shape=outs,
        in_specs=[pl.BlockSpec(memory_space=pltpu.VMEM)] * len(args),
        out_specs=jax.tree.map(lambda _: pl.BlockSpec(memory_space=pltpu.VMEM), outs),
        scratch_shapes=scratch,
        compiler_params=pltpu.CompilerParams(vmem_limit_bytes=32 * 1024 * 1024),
        cost_estimate=pl.CostEstimate(flops=cost, bytes_accessed=1 << 20, transcendentals=0),
    )(*args)


def swap(x, partner):
    places = range(lax.axis_size("row") * lax.axis_size("col"))
    return lax.ppermute(x, ("row", "col"), [(i, partner(i)) for i in places])


def exchange_cols(first, second):
    across = lax.axis_size("col")

    def after_odd(i):
        row, col = i // across, i % across
        return row * across + (((col - 1) % across ^ 1) + 1) % across

    second = swap(second, after_odd)
    return swap(first, lambda i: i ^ 1), second


def exchange_rows(first, second):
    across, down = lax.axis_size("col"), lax.axis_size("row")

    def after_odd(i):
        row, col = i // across, i % across
        return i ^ 1 if row in (0, down - 1) else (((row - 1) ^ 1) + 1) * across + col

    return swap(first, lambda i: (i // across ^ 1) * across + i % across), swap(second, after_odd)


def sum_everywhere(part, work, *args):
    across, down = lax.axis_size("col"), lax.axis_size("row")
    beside = list(range(1, across.bit_length() - 1))
    below = list(range(across.bit_length() - 1, (across * down).bit_length() - 1))
    turns = [(beside[n : n + 1], below[n : n + 1]) for n in range(max(len(beside), len(below)))]
    even = [bit for a, b in turns for bit in a + b]
    odd = [bit for a, b in turns for bit in b + a]
    for n, bits in enumerate(zip(even, odd)):
        message = lax.optimization_barrier(lax.reduce_precision(part, 5, 10).astype(jnp.float16))
        received = swap(message, lambda i: i ^ (1 << bits[i.bit_count() % 2]) ^ 1)
        if n == 0:
            _, *args = lax.optimization_barrier((message, *args))
            received, done = lax.optimization_barrier((received, work(*args)))
        rows = part.shape[0] - (NOTES if n == len(even) - 1 else 0)
        part = call(
            add_kernel, jax.ShapeDtypeStruct((rows, part.shape[1]), F32), [], 1 << 16,
            message.astype(F32), received.astype(F32),
        )
    return part, swap(part, lambda i: i ^ 1), done


def body(feature, cotangent, order_weight, pixel_mask):
    orders, channels, _ = order_weight.shape
    _, rows, cols = feature.shape
    half, lanes, halo = cols // 2, 2 * channels, orders - 1
    tall, total = half + 2 * RIM, rows + 2 * halo
    shape = jax.ShapeDtypeStruct
    wide = pltpu.VMEM((channels * rows, cols), F32)
    marks = shape((2 * rows, cols), BF16)

    mask16 = call(mask_kernel, marks, [], 1 << 31, pixel_mask)
    sent = shape((halo * half + 2 * rows, lanes), BF16)
    cot_body, first, second = call(
        functools.partial(pack_kernel, halo), [shape((rows * half, lanes), BF16), sent, sent], [wide], 1 << 20,
        cotangent, mask16,
    )
    first, second = exchange_rows(first, second)
    features, rims, weights = call(
        early_kernel,
        [shape((lanes, rows * half), BF16), shape((lanes, rows * RIM), BF16), shape((lanes, orders * lanes), BF16)],
        [wide], 1 << 20, feature, order_weight,
    )
    sent = shape((-(-(3 * rows + total // 2 * RIM) // 16) * 16, lanes), BF16)
    west_first, west_second = call(
        functools.partial(strips_kernel, halo), [sent, sent], [], 1 << 16, cot_body, mask16, second, first
    )
    west_first, west_second = exchange_cols(west_first, west_second)
    buffer = pltpu.VMEM((total * tall, lanes), F32)
    small = pltpu.VMEM((total * 3 * RIM, lanes), F32)
    terms = shape((rows * half, orders * lanes), BF16)
    rim_terms = shape((rows * RIM, orders * lanes), BF16)
    inner, sums, own, centre = call(
        functools.partial(interior_kernel, orders),
        [
            terms, shape((orders // 2, channels, lanes), F32), shape((total * 3 * RIM, lanes), F32),
            shape((3 * rows, cols), F32),
        ],
        [buffer, buffer, buffer], 1 << 28, cot_body, mask16, second, first, features,
    )
    outer, message = call(
        functools.partial(edge_kernel, orders), [rim_terms, shape((orders // 2 * channels + NOTES, lanes), F32)],
        [small, small, small, pltpu.VMEM(rim_terms.shape, F32)], 1 << 26,
        own, centre, west_second, west_first, rims, sums,
    )
    mix = functools.partial(
        call, mix_kernel, shape((channels, rows, cols), BF16), [wide, pltpu.VMEM(terms.shape, BF16)], 1 << 20
    )
    mine, other, grad_feature = sum_everywhere(message, mix, weights, inner, outer)
    pixel_count = rows * cols * lax.axis_size("row") * lax.axis_size("col")
    grad_order = call(
        functools.partial(finish_kernel, math.sqrt(pixel_count)),
        shape((orders, channels, channels), F32), [], 1 << 16, mine, other,
    )
    return (grad_feature, grad_order)


def solution(mesh):
    placed = (P(None, "row", "col"), P(None, "row", "col"), P(), P("row", "col"))
    return jax.shard_map(
        body, mesh=mesh, in_specs=placed, out_specs=(P(None, "row", "col"), P()), check_vma=False
    )
```

```python
import functools
import math

import jax
import jax.numpy as jnp
from jax import lax
from jax.experimental import pallas as pl
from jax.experimental.pallas import tpu as pltpu
from jax.sharding import PartitionSpec as P

RIM = 8
NOTES = 16
F32 = jnp.float32
BF16 = jnp.bfloat16
NT = (((1,), (1,)), ((), ()))


def iota(shape, dim):
    return lax.broadcasted_iota(jnp.int32, shape, dim)


def swap_halves(x):
    return pltpu.roll(x, x.shape[-1] // 2, x.ndim - 1)


def even_place(axis):
    return lax.axis_index(axis) % 2 == 0


def in_order(axis, first, second):
    even, place = even_place(axis), lax.axis_index(axis)
    before, after = jnp.where(even, second, first), jnp.where(even, first, second)
    return jnp.where(place == 0, 0.0, before), jnp.where(place == lax.axis_size(axis) - 1, 0.0, after)


def mask_kernel(mask_ref, out_ref):
    mask = mask_ref[...].astype(F32)
    out_ref[...] = jnp.concatenate([mask, jnp.zeros_like(mask)], axis=0).astype(BF16)


def pack_kernel(halo, cot_ref, mask_ref, body_ref, first_ref, second_ref, wide_ref):
    channels, rows, cols = cot_ref.shape
    half, lanes = cols // 2, 2 * channels
    wide_ref[...] = cot_ref[...].astype(F32).reshape(channels * rows, cols)
    fold = (iota((half, cols), 1) % half == iota((half, cols), 0)).astype(BF16)
    left = iota((channels, cols), 1) < half
    stacked = []
    for r in range(rows):
        row = wide_ref[pl.ds(r, channels, stride=rows), :]
        stacked += [jnp.where(left, row, 0.0), jnp.where(left, 0.0, row)]
    stacked = jnp.concatenate(stacked, axis=0).astype(BF16)
    body = lax.dot_general(fold, stacked, NT, preferred_element_type=F32)
    for r in range(rows):
        body_ref[r * half : (r + 1) * half, :] = body[:, r * lanes : (r + 1) * lanes].astype(BF16)
    south, count = even_place("row"), halo * half
    for out_ref, lower in ((first_ref, south), (second_ref, jnp.logical_not(south))):
        start = pl.multiple_of(jnp.where(lower, rows * half - count, 0), half)
        out_ref[:count, :] = body_ref[pl.ds(start, count), :]
        out_ref[count:, :] = mask_ref[...]


def early_kernel(feature_ref, weight_ref, feature_out_ref, rim_out_ref, weight_out_ref, wide_ref):
    channels, rows, cols = feature_ref.shape
    lanes = 2 * channels
    wide_ref[...] = feature_ref[...].astype(F32).reshape(channels * rows, cols)
    left = iota((channels, cols), 1) < cols // 2
    for q in range(rows // 2):
        even = wide_ref[pl.ds(2 * q, channels, stride=rows), :]
        odd = wide_ref[pl.ds(2 * q + 1, channels, stride=rows), :]
        at = slice(q * cols, (q + 1) * cols)
        feature_out_ref[:channels, at] = jnp.where(left, even, swap_halves(odd)).astype(BF16)
        feature_out_ref[channels:, at] = jnp.where(left, swap_halves(even), odd).astype(BF16)
    half, shape = cols // 2, (rows * cols // 2, rows * RIM)
    pixel, target = iota(shape, 0), iota(shape, 1)
    here = target // RIM * half + target % RIM
    sides = [
        jnp.dot(feature_out_ref[...], (pixel == here + skip).astype(BF16), preferred_element_type=F32)
        for skip in (0, half - RIM)
    ]
    rim_out_ref[:channels, :] = sides[0][:channels].astype(BF16)
    rim_out_ref[channels:, :] = sides[1][channels:].astype(BF16)
    for k in range(weight_ref.shape[0]):
        weight = weight_ref[k].astype(F32) * (-1.0) ** k
        blank = jnp.zeros_like(weight)
        at = slice(k * lanes, (k + 1) * lanes)
        weight_out_ref[:channels, at] = jnp.concatenate([weight, blank], axis=1).astype(BF16)
        weight_out_ref[channels:, at] = jnp.concatenate([blank, weight], axis=1).astype(BF16)


def row_pieces(halo, half, body_ref, first_ref, second_ref, begin, size):
    rows = body_ref.shape[0] // half

    def piece(ref, r):
        return ref[r * half + begin : r * half + begin + size, :].astype(F32)

    received = [in_order("row", piece(first_ref, r), piece(second_ref, r)) for r in range(halo)]
    return [north for north, _ in received] + [piece(body_ref, r) for r in range(rows)] + [south for _, south in received]


def all_masks(halo, half, mask_ref, first_ref, second_ref):
    rows, begin = mask_ref.shape[0] // 2, halo * half
    north, south = in_order("row", first_ref[begin:, :].astype(F32), second_ref[begin:, :].astype(F32))
    return jnp.concatenate([north[:rows], mask_ref[...].astype(F32)[:rows], south[:rows]], axis=0)


def edge_lanes(masks):
    cols = masks.shape[1]
    return pltpu.roll(masks, cols // 4, 1), pltpu.roll(masks, cols - cols // 4, 1)


def strips_kernel(halo, body_ref, mask_ref, second_ref, first_ref, to_first_ref, to_second_ref):
    rows = mask_ref.shape[0] // 2
    half = body_ref.shape[0] // rows
    total = rows + 2 * halo
    marks = 3 * rows
    masks = all_masks(halo, half, mask_ref, first_ref, second_ref)
    ahead, behind = edge_lanes(masks)
    leading = row_pieces(halo, half, body_ref, first_ref, second_ref, 0, 2 * RIM)
    trailing = row_pieces(halo, half, body_ref, first_ref, second_ref, half - 2 * RIM, 2 * RIM)
    low = iota((RIM, body_ref.shape[1]), 1) < body_ref.shape[1] // 2
    west, east = [], []
    for n in range(total // 2):
        west.append(jnp.where(low, leading[n][:RIM], swap_halves(leading[n + total // 2][:RIM])))
        east.append(jnp.where(low, swap_halves(trailing[n][RIM:]), trailing[n + total // 2][RIM:]))
    spare = to_first_ref.shape[0] - total // 2 * RIM - marks
    blank = [jnp.zeros((spare, body_ref.shape[1]), F32)] if spare else []
    west, east = (jnp.concatenate([marks_sent, *x] + blank, axis=0) for marks_sent, x in ((behind, west), (ahead, east)))
    even = even_place("col")
    to_first_ref[...] = jnp.where(even, east, west).astype(BF16)
    to_second_ref[...] = jnp.where(even, west, east).astype(BF16)


def compact_scales(mask):
    rows, cols = mask.shape
    column = mask + pltpu.roll(mask, 1, 0) + pltpu.roll(mask, rows - 1, 0)
    degree = mask * (column + pltpu.roll(column, 1, 1) + pltpu.roll(column, cols - 1, 1) - mask)
    return jnp.transpose(mask * lax.rsqrt(jnp.maximum(0.5 * degree, 0.5)), (1, 0))


def spread_scales(left, right, scale_ref):
    (tall, marks), lanes = left.shape, scale_ref.shape[1]
    total = scale_ref.shape[0] // tall
    spare = jnp.zeros((tall, lanes // 2 - marks), F32)
    both = jnp.concatenate([left, spare, right, spare], axis=1)
    lane = iota((tall, lanes), 1)
    start = jnp.where(lane < lanes // 2, 0, lanes // 2) + (marks - total) // 2
    for q in range(total):
        picked = jnp.take_along_axis(both, start + q, axis=1, mode="promise_in_bounds")
        scale_ref[q * tall : (q + 1) * tall, :] = picked


def next_term(k, tall, scale_ref, newer_ref, older_ref, visit):
    total = scale_ref.shape[0] // tall

    def at(q):
        return slice(q * tall, (q + 1) * tall)

    def weighted(q):
        return scale_ref[at(q), :] * newer_ref[at(q), :]

    above, here = weighted(k - 1), weighted(k)
    for q in range(k, total - k):
        below = weighted(q + 1)
        column = above + here + below
        nearby = column + pltpu.roll(column, 1, 0) + pltpu.roll(column, tall - 1, 0) - here
        fresh = scale_ref[at(q), :] * nearby
        fresh = 0.5 * fresh if k == 1 else fresh - older_ref[at(q), :]
        older_ref[at(q), :] = fresh
        visit(q, fresh)
        above, here = here, below


def order_products(lanes, feature, terms):
    channels = lanes // 2
    product = jnp.dot(feature, terms, preferred_element_type=F32)
    near, far = product[:channels], product[channels:]
    even = near[:, :lanes] + swap_halves(far[:, :lanes])
    odd = swap_halves(near[:, lanes:]) + far[:, lanes:]
    return jnp.where(iota((channels, lanes), 1) < channels, even, -odd)


def interior_kernel(
    orders, body_ref, mask_ref, second_ref, first_ref, feature_ref, terms_ref, sums_ref, own_ref, centre_ref, even_ref, odd_ref, scale_ref
):
    rows, cols = mask_ref.shape[0] // 2, mask_ref.shape[1]
    half, halo, lanes = cols // 2, orders - 1, body_ref.shape[1]
    tall = half + 2 * RIM
    masks = all_masks(halo, half, mask_ref, first_ref, second_ref)
    ahead, behind = edge_lanes(masks)
    centre_ref[...] = jnp.where(iota(masks.shape, 1) < half, ahead, behind)
    across = compact_scales(masks)
    rim = jnp.zeros((RIM, across.shape[1]), F32)
    left = jnp.concatenate([rim, across[: half + RIM]], axis=0)
    right = jnp.concatenate([across[half - RIM :], rim], axis=0)
    spread_scales(left, right, scale_ref)
    low = iota((RIM, lanes), 1) < lanes // 2
    for q, middle in enumerate(row_pieces(halo, half, body_ref, first_ref, second_ref, 0, half)):
        at = q * tall
        odd_ref[at : at + RIM, :] = jnp.where(low, 0.0, swap_halves(middle[half - RIM :]))
        odd_ref[at + RIM : at + RIM + half, :] = middle
        odd_ref[at + RIM + half : at + tall, :] = jnp.where(low, swap_halves(middle[:RIM]), 0.0)
        at = q * 3 * RIM
        tail = half - 2 * RIM
        own_ref[at : at + RIM, :] = jnp.where(low, 0.0, middle[tail : tail + RIM])
        own_ref[at + RIM : at + 2 * RIM, :] = jnp.where(low, middle[:RIM], middle[tail + RIM :])
        own_ref[at + 2 * RIM : at + 3 * RIM, :] = jnp.where(low, middle[RIM : 2 * RIM], 0.0)
    terms_ref[:, :lanes] = body_ref[...]
    newer, older = odd_ref, even_ref
    for k in range(1, orders):
        def keep(q, fresh):
            r = q - halo
            if 0 <= r < rows:
                columns = slice(k * lanes, (k + 1) * lanes)
                first = jnp.where(low, 0.0, fresh[RIM : 2 * RIM])
                last = jnp.where(low, fresh[half : half + RIM], 0.0)
                kept = jnp.concatenate([first, fresh[2 * RIM : half], last], axis=0)
                terms_ref[r * half : (r + 1) * half, columns] = kept.astype(BF16)

        next_term(k, tall, scale_ref, newer, older, keep)
        newer, older = older, newer
        if k % 2:
            pair = slice((k - 1) * lanes, (k + 1) * lanes)
            sums_ref[k // 2] = order_products(lanes, feature_ref[...], terms_ref[:, pair])


def store_sums(message_ref, blocks, exponent):
    scale, at = jnp.exp2(9.0 - exponent), 0
    for block in blocks:
        for row in range(0, block.shape[0], 8):
            message_ref[at : at + 8, :] = block[row : row + 8] * scale
            at += 8
    message_ref[at:, :] = jnp.concatenate([exponent] * (NOTES // 8), axis=0)


def add_kernel(mine_ref, received_ref, out_ref):
    notes = mine_ref.shape[0] - NOTES
    mine, received = mine_ref[notes : notes + 8, :], received_ref[notes : notes + 8, :]
    scales = jnp.exp2(mine - 9.0), jnp.exp2(received - 9.0)
    sums = []
    for row in range(0, notes, 8):
        at = slice(row, row + 8)
        sums.append(mine_ref[at, :] * scales[0] + received_ref[at, :] * scales[1])
    if out_ref.shape[0] == notes:
        out_ref[...] = jnp.concatenate(sums, axis=0)
    else:
        store_sums(out_ref, sums, jnp.maximum(mine, received) + 1.0)


def edge_kernel(
    orders, own_ref, centre_ref, second_ref, first_ref, rim_ref, sums_ref,
    terms_ref, message_ref, even_ref, odd_ref, scale_ref, wide_ref,
):
    rows, cols = centre_ref.shape[0] // 3, centre_ref.shape[1]
    halo, lanes, quarter = orders - 1, own_ref.shape[1], cols // 4
    channels, total, tall = lanes // 2, rows + 2 * halo, 3 * RIM
    west, east = in_order("col", first_ref[...].astype(F32), second_ref[...].astype(F32))
    lane = iota((3 * rows, cols), 1)
    masks = jnp.where(lane < quarter, west[: 3 * rows], jnp.where(lane < 3 * quarter, centre_ref[...], east[: 3 * rows]))
    across = compact_scales(masks)
    begin = quarter - RIM
    spread_scales(across[begin : begin + tall], across[3 * quarter - 2 * RIM : 3 * quarter + RIM], scale_ref)

    low = iota((RIM, lanes), 1) < channels
    for q in range(total):
        n, upper_row = q % (total // 2), q >= total // 2
        strip = slice(3 * rows + n * RIM, 3 * rows + (n + 1) * RIM)
        before = swap_halves(west[strip]) if upper_row else west[strip]
        after = east[strip] if upper_row else swap_halves(east[strip])
        at = q * tall
        odd_ref[at : at + RIM, :] = jnp.where(low, before, own_ref[at : at + RIM, :])
        odd_ref[at + RIM : at + 2 * RIM, :] = own_ref[at + RIM : at + 2 * RIM, :]
        odd_ref[at + 2 * RIM : at + tall, :] = jnp.where(low, own_ref[at + 2 * RIM : at + tall, :], after)

    wide_ref[:, :lanes] = jnp.zeros((rows * RIM, lanes), F32)
    blocks = []
    newer, older = odd_ref, even_ref
    for k in range(1, orders):
        def keep(q, fresh):
            r = q - halo
            if 0 <= r < rows:
                wide_ref[r * RIM : (r + 1) * RIM, k * lanes : (k + 1) * lanes] = fresh[RIM : 2 * RIM]

        next_term(k, tall, scale_ref, newer, older, keep)
        newer, older = older, newer
        if k % 2:
            pair = slice((k - 1) * lanes, (k + 1) * lanes)
            terms = wide_ref[:, pair].astype(BF16)
            terms_ref[:, pair] = terms
            blocks.append(sums_ref[k // 2] + order_products(lanes, rim_ref[...], terms))
    tiles = [jnp.abs(block[row : row + 8]) for block in blocks for row in range(0, channels, 8)]
    largest = functools.reduce(jnp.maximum, tiles)
    exponent = jnp.floor(jnp.log2(jnp.maximum(largest, 1e-30))) + 1.0
    store_sums(message_ref, blocks, exponent)


def mix_kernel(weight_ref, inner_ref, rim_ref, grad_ref, wide_ref, terms_ref):
    channels, rows, cols = grad_ref.shape
    half, lanes = cols // 2, 2 * channels
    terms_ref[...] = inner_ref[...]
    lane, sublane = iota((2 * RIM, lanes), 1), iota((2 * RIM, lanes), 0)
    first_columns = jnp.logical_and(lane < channels, sublane < RIM)
    last_columns = jnp.logical_and(lane >= channels, sublane >= RIM)
    for k in range(1, rim_ref.shape[1] // lanes):
        columns = slice(k * lanes, (k + 1) * lanes)
        rims = rim_ref[:, columns].astype(F32)
        for r in range(rows):
            twice = jnp.concatenate([rims[r * RIM : (r + 1) * RIM]] * 2, axis=0)
            for begin, chosen in ((r * half, first_columns), ((r + 1) * half - 2 * RIM, last_columns)):
                at = (slice(begin, begin + 2 * RIM), columns)
                terms_ref[at] = jnp.where(chosen, twice, inner_ref[at].astype(F32)).astype(BF16)
    low = iota((channels, cols), 1) < half
    mixed = lax.dot_general(weight_ref[...], terms_ref[...], NT, preferred_element_type=F32)
    for q in range(rows // 2):
        upper, lower = mixed[:channels, q * cols : (q + 1) * cols], mixed[channels:, q * cols : (q + 1) * cols]
        wide_ref[pl.ds(2 * q, channels, stride=rows), :] = jnp.where(low, upper, swap_halves(lower))
        wide_ref[pl.ds(2 * q + 1, channels, stride=rows), :] = jnp.where(low, swap_halves(upper), lower)
    grad_ref[...] = wide_ref[...].reshape(channels, rows, cols).astype(BF16)


def finish_kernel(divisor, mine_ref, other_ref, out_ref):
    channels = out_ref.shape[1]
    for b in range(out_ref.shape[0] // 2):
        at = slice(b * channels, (b + 1) * channels)
        block = (mine_ref[at, :] + other_ref[at, :]) / divisor
        out_ref[2 * b] = block[:, :channels]
        out_ref[2 * b + 1] = block[:, channels:]


def call(kernel, outs, scratch, cost, *args):
    return pl.pallas_call(
        kernel,
        out_shape=outs,
        in_specs=[pl.BlockSpec(memory_space=pltpu.VMEM)] * len(args),
        out_specs=jax.tree.map(lambda _: pl.BlockSpec(memory_space=pltpu.VMEM), outs),
        scratch_shapes=scratch,
        compiler_params=pltpu.CompilerParams(vmem_limit_bytes=32 * 1024 * 1024),
        cost_estimate=pl.CostEstimate(flops=cost, bytes_accessed=1 << 20, transcendentals=0),
    )(*args)


def swap(x, partner):
    places = range(lax.axis_size("row") * lax.axis_size("col"))
    return lax.ppermute(x, ("row", "col"), [(i, partner(i)) for i in places])


def exchange_cols(first, second):
    across = lax.axis_size("col")

    def after_odd(i):
        row, col = i // across, i % across
        return row * across + (((col - 1) % across ^ 1) + 1) % across

    second = swap(second, after_odd)
    return swap(first, lambda i: i ^ 1), second


def exchange_rows(first, second):
    across, down = lax.axis_size("col"), lax.axis_size("row")

    def after_odd(i):
        row, col = i // across, i % across
        return i ^ 1 if row in (0, down - 1) else (((row - 1) ^ 1) + 1) * across + col

    return swap(first, lambda i: (i // across ^ 1) * across + i % across), swap(second, after_odd)


def sum_everywhere(part, work, *args):
    across, down = lax.axis_size("col"), lax.axis_size("row")
    beside = list(range(1, across.bit_length() - 1))
    below = list(range(across.bit_length() - 1, (across * down).bit_length() - 1))
    turns = [(beside[n : n + 1], below[n : n + 1]) for n in range(max(len(beside), len(below)))]
    even = [bit for a, b in turns for bit in a + b]
    odd = [bit for a, b in turns for bit in b + a]
    for n, bits in enumerate(zip(even, odd)):
        message = lax.optimization_barrier(part.astype(jnp.float16))
        received = swap(message, lambda i: i ^ (1 << bits[i.bit_count() % 2]) ^ 1)
        if n == 0:
            _, *args = lax.optimization_barrier((message, *args))
            received, done = lax.optimization_barrier((received, work(*args)))
        rows = part.shape[0] - (NOTES if n == len(even) - 1 else 0)
        part = call(
            add_kernel, jax.ShapeDtypeStruct((rows, part.shape[1]), F32), [], 1 << 16,
            message.astype(F32), received.astype(F32),
        )
    return part, swap(part, lambda i: i ^ 1), done


def body(feature, cotangent, order_weight, pixel_mask):
    orders, channels, _ = order_weight.shape
    _, rows, cols = feature.shape
    half, lanes, halo = cols // 2, 2 * channels, orders - 1
    tall, total = half + 2 * RIM, rows + 2 * halo
    shape = jax.ShapeDtypeStruct
    wide = pltpu.VMEM((channels * rows, cols), F32)
    marks = shape((2 * rows, cols), BF16)

    mask16 = call(mask_kernel, marks, [], 1 << 31, pixel_mask)
    sent = shape((halo * half + 2 * rows, lanes), BF16)
    cot_body, first, second = call(
        functools.partial(pack_kernel, halo), [shape((rows * half, lanes), BF16), sent, sent], [wide], 1 << 20,
        cotangent, mask16,
    )
    first, second = exchange_rows(first, second)
    features, rims, weights = call(
        early_kernel,
        [shape((lanes, rows * half), BF16), shape((lanes, rows * RIM), BF16), shape((lanes, orders * lanes), BF16)],
        [wide], 1 << 20, feature, order_weight,
    )
    sent = shape((-(-(3 * rows + total // 2 * RIM) // 16) * 16, lanes), BF16)
    west_first, west_second = call(
        functools.partial(strips_kernel, halo), [sent, sent], [], 1 << 16, cot_body, mask16, second, first
    )
    west_first, west_second = exchange_cols(west_first, west_second)
    buffer = pltpu.VMEM((total * tall, lanes), F32)
    small = pltpu.VMEM((total * 3 * RIM, lanes), F32)
    terms = shape((rows * half, orders * lanes), BF16)
    rim_terms = shape((rows * RIM, orders * lanes), BF16)
    inner, sums, own, centre = call(
        functools.partial(interior_kernel, orders),
        [
            terms, shape((orders // 2, channels, lanes), F32), shape((total * 3 * RIM, lanes), F32),
            shape((3 * rows, cols), F32),
        ],
        [buffer, buffer, buffer], 1 << 28, cot_body, mask16, second, first, features,
    )
    outer, message = call(
        functools.partial(edge_kernel, orders), [rim_terms, shape((orders // 2 * channels + NOTES, lanes), F32)],
        [small, small, small, pltpu.VMEM(rim_terms.shape, F32)], 1 << 26,
        own, centre, west_second, west_first, rims, sums,
    )
    mix = functools.partial(
        call, mix_kernel, shape((channels, rows, cols), BF16), [wide, pltpu.VMEM(terms.shape, BF16)], 1 << 20
    )
    mine, other, grad_feature = sum_everywhere(message, mix, weights, inner, outer)
    pixel_count = rows * cols * lax.axis_size("row") * lax.axis_size("col")
    grad_order = call(
        functools.partial(finish_kernel, math.sqrt(pixel_count)),
        shape((orders, channels, channels), F32), [], 1 << 16, mine, other,
    )
    return (grad_feature, grad_order)


def solution(mesh):
    placed = (P(None, "row", "col"), P(None, "row", "col"), P(), P("row", "col"))
    return jax.shard_map(
        body, mesh=mesh, in_specs=placed, out_specs=(P(None, "row", "col"), P()), check_vma=False
    )
```

```python
import functools
import math

import jax
import jax.numpy as jnp
from jax import lax
from jax.experimental import pallas as pl
from jax.experimental.pallas import tpu as pltpu
from jax.sharding import PartitionSpec as P

RIM = 8
NOTES = 16
F32 = jnp.float32
BF16 = jnp.bfloat16
NT = (((1,), (1,)), ((), ()))


def iota(shape, dim):
    return lax.broadcasted_iota(jnp.int32, shape, dim)


def swap_halves(x):
    return pltpu.roll(x, x.shape[-1] // 2, x.ndim - 1)


def even_place(axis):
    return lax.axis_index(axis) % 2 == 0


def in_order(axis, first, second):
    even, place = even_place(axis), lax.axis_index(axis)
    before, after = jnp.where(even, second, first), jnp.where(even, first, second)
    return jnp.where(place == 0, 0.0, before), jnp.where(place == lax.axis_size(axis) - 1, 0.0, after)


def mask_kernel(mask_ref, out_ref):
    mask = mask_ref[...].astype(F32)
    out_ref[...] = jnp.concatenate([mask, jnp.zeros_like(mask)], axis=0).astype(BF16)


def pack_kernel(halo, cot_ref, mask_ref, body_ref, first_ref, second_ref, wide_ref):
    channels, rows, cols = cot_ref.shape
    half, lanes = cols // 2, 2 * channels
    wide_ref[...] = cot_ref[...].astype(F32).reshape(channels * rows, cols)
    fold = (iota((half, cols), 1) % half == iota((half, cols), 0)).astype(BF16)
    left = iota((channels, cols), 1) < half
    stacked = []
    for r in range(rows):
        row = wide_ref[pl.ds(r, channels, stride=rows), :]
        stacked += [jnp.where(left, row, 0.0), jnp.where(left, 0.0, row)]
    stacked = jnp.concatenate(stacked, axis=0).astype(BF16)
    body = lax.dot_general(fold, stacked, NT, preferred_element_type=F32)
    for r in range(rows):
        body_ref[r * half : (r + 1) * half, :] = body[:, r * lanes : (r + 1) * lanes].astype(BF16)
    south, count = even_place("row"), halo * half
    for out_ref, lower in ((first_ref, south), (second_ref, jnp.logical_not(south))):
        start = pl.multiple_of(jnp.where(lower, rows * half - count, 0), half)
        out_ref[:count, :] = body_ref[pl.ds(start, count), :]
        out_ref[count:, :] = mask_ref[...]


def early_kernel(feature_ref, weight_ref, feature_out_ref, rim_out_ref, weight_out_ref, wide_ref):
    channels, rows, cols = feature_ref.shape
    lanes = 2 * channels
    wide_ref[...] = feature_ref[...].astype(F32).reshape(channels * rows, cols)
    left = iota((channels, cols), 1) < cols // 2
    for q in range(rows // 2):
        even = wide_ref[pl.ds(2 * q, channels, stride=rows), :]
        odd = wide_ref[pl.ds(2 * q + 1, channels, stride=rows), :]
        at = slice(q * cols, (q + 1) * cols)
        feature_out_ref[:channels, at] = jnp.where(left, even, swap_halves(odd)).astype(BF16)
        feature_out_ref[channels:, at] = jnp.where(left, swap_halves(even), odd).astype(BF16)
    half, shape = cols // 2, (rows * cols // 2, rows * RIM)
    pixel, target = iota(shape, 0), iota(shape, 1)
    here = target // RIM * half + target % RIM
    sides = [
        jnp.dot(feature_out_ref[...], (pixel == here + skip).astype(BF16), preferred_element_type=F32)
        for skip in (0, half - RIM)
    ]
    rim_out_ref[:channels, :] = sides[0][:channels].astype(BF16)
    rim_out_ref[channels:, :] = sides[1][channels:].astype(BF16)
    for k in range(weight_ref.shape[0]):
        weight = weight_ref[k].astype(F32) * (-1.0) ** k
        blank = jnp.zeros_like(weight)
        at = slice(k * lanes, (k + 1) * lanes)
        weight_out_ref[:channels, at] = jnp.concatenate([weight, blank], axis=1).astype(BF16)
        weight_out_ref[channels:, at] = jnp.concatenate([blank, weight], axis=1).astype(BF16)


def row_pieces(halo, half, body_ref, first_ref, second_ref, begin, size):
    rows = body_ref.shape[0] // half

    def piece(ref, r):
        return ref[r * half + begin : r * half + begin + size, :].astype(F32)

    received = [in_order("row", piece(first_ref, r), piece(second_ref, r)) for r in range(halo)]
    return [north for north, _ in received] + [piece(body_ref, r) for r in range(rows)] + [south for _, south in received]


def all_masks(halo, half, mask_ref, first_ref, second_ref):
    rows, begin = mask_ref.shape[0] // 2, halo * half
    north, south = in_order("row", first_ref[begin:, :].astype(F32), second_ref[begin:, :].astype(F32))
    return jnp.concatenate([north[:rows], mask_ref[...].astype(F32)[:rows], south[:rows]], axis=0)


def edge_lanes(masks):
    cols = masks.shape[1]
    return pltpu.roll(masks, cols // 4, 1), pltpu.roll(masks, cols - cols // 4, 1)


def strips_kernel(halo, body_ref, mask_ref, second_ref, first_ref, to_first_ref, to_second_ref):
    rows = mask_ref.shape[0] // 2
    half = body_ref.shape[0] // rows
    total = rows + 2 * halo
    marks = 3 * rows
    masks = all_masks(halo, half, mask_ref, first_ref, second_ref)
    ahead, behind = edge_lanes(masks)
    leading = row_pieces(halo, half, body_ref, first_ref, second_ref, 0, 2 * RIM)
    trailing = row_pieces(halo, half, body_ref, first_ref, second_ref, half - 2 * RIM, 2 * RIM)
    low = iota((RIM, body_ref.shape[1]), 1) < body_ref.shape[1] // 2
    west, east = [], []
    for n in range(total // 2):
        west.append(jnp.where(low, leading[n][:RIM], swap_halves(leading[n + total // 2][:RIM])))
        east.append(jnp.where(low, swap_halves(trailing[n][RIM:]), trailing[n + total // 2][RIM:]))
    spare = to_first_ref.shape[0] - total // 2 * RIM - marks
    blank = [jnp.zeros((spare, body_ref.shape[1]), F32)] if spare else []
    west, east = (jnp.concatenate([marks_sent, *x] + blank, axis=0) for marks_sent, x in ((behind, west), (ahead, east)))
    even = even_place("col")
    to_first_ref[...] = jnp.where(even, east, west).astype(BF16)
    to_second_ref[...] = jnp.where(even, west, east).astype(BF16)


def compact_scales(mask):
    rows, cols = mask.shape
    column = mask + pltpu.roll(mask, 1, 0) + pltpu.roll(mask, rows - 1, 0)
    degree = mask * (column + pltpu.roll(column, 1, 1) + pltpu.roll(column, cols - 1, 1) - mask)
    return jnp.transpose(mask * lax.rsqrt(jnp.maximum(0.5 * degree, 0.5)), (1, 0))


def spread_scales(left, right, scale_ref):
    (tall, marks), lanes = left.shape, scale_ref.shape[1]
    total = scale_ref.shape[0] // tall
    spare = jnp.zeros((tall, lanes // 2 - marks), F32)
    both = jnp.concatenate([left, spare, right, spare], axis=1)
    lane = iota((tall, lanes), 1)
    start = jnp.where(lane < lanes // 2, 0, lanes // 2) + (marks - total) // 2
    for q in range(total):
        picked = jnp.take_along_axis(both, start + q, axis=1, mode="promise_in_bounds")
        scale_ref[q * tall : (q + 1) * tall, :] = picked


def next_term(k, tall, scale_ref, newer_ref, older_ref, shift_ref, visit):
    total = scale_ref.shape[0] // tall

    def at(q):
        return slice(q * tall, (q + 1) * tall)

    def weighted(q):
        return scale_ref[at(q), :] * newer_ref[at(q), :]

    above, here = weighted(k - 1), weighted(k)
    for q in range(k, total - k):
        below = weighted(q + 1)
        beside = above + below
        column = beside + here
        begin = q * (tall + 2 * RIM) + RIM
        shift_ref[begin : begin + tall, :] = column
        nearby = beside + shift_ref[begin - 1 : begin - 1 + tall, :] + shift_ref[begin + 1 : begin + 1 + tall, :]
        fresh = scale_ref[at(q), :] * nearby
        fresh = 0.5 * fresh if k == 1 else fresh - older_ref[at(q), :]
        older_ref[at(q), :] = fresh
        visit(q, fresh)
        above, here = here, below


def order_products(lanes, feature, terms):
    channels = lanes // 2
    product = jnp.dot(feature, terms, preferred_element_type=F32)
    near, far = product[:channels], product[channels:]
    even = near[:, :lanes] + swap_halves(far[:, :lanes])
    odd = swap_halves(near[:, lanes:]) + far[:, lanes:]
    return jnp.where(iota((channels, lanes), 1) < channels, even, -odd)


def interior_kernel(
    orders, body_ref, mask_ref, second_ref, first_ref, feature_ref, terms_ref, sums_ref, own_ref, centre_ref, even_ref, odd_ref, scale_ref, shift_ref
):
    rows, cols = mask_ref.shape[0] // 2, mask_ref.shape[1]
    half, halo, lanes = cols // 2, orders - 1, body_ref.shape[1]
    tall = half + 2 * RIM
    masks = all_masks(halo, half, mask_ref, first_ref, second_ref)
    ahead, behind = edge_lanes(masks)
    centre_ref[...] = jnp.where(iota(masks.shape, 1) < half, ahead, behind)
    across = compact_scales(masks)
    rim = jnp.zeros((RIM, across.shape[1]), F32)
    left = jnp.concatenate([rim, across[: half + RIM]], axis=0)
    right = jnp.concatenate([across[half - RIM :], rim], axis=0)
    spread_scales(left, right, scale_ref)
    low = iota((RIM, lanes), 1) < lanes // 2
    for q, middle in enumerate(row_pieces(halo, half, body_ref, first_ref, second_ref, 0, half)):
        at = q * tall
        odd_ref[at : at + RIM, :] = jnp.where(low, 0.0, swap_halves(middle[half - RIM :]))
        odd_ref[at + RIM : at + RIM + half, :] = middle
        odd_ref[at + RIM + half : at + tall, :] = jnp.where(low, swap_halves(middle[:RIM]), 0.0)
        at = q * 3 * RIM
        tail = half - 2 * RIM
        own_ref[at : at + RIM, :] = jnp.where(low, 0.0, middle[tail : tail + RIM])
        own_ref[at + RIM : at + 2 * RIM, :] = jnp.where(low, middle[:RIM], middle[tail + RIM :])
        own_ref[at + 2 * RIM : at + 3 * RIM, :] = jnp.where(low, middle[RIM : 2 * RIM], 0.0)
    terms_ref[:, :lanes] = body_ref[...]
    shift_ref[...] = jnp.zeros_like(shift_ref)
    newer, older = odd_ref, even_ref
    for k in range(1, orders):
        def keep(q, fresh):
            r = q - halo
            if 0 <= r < rows:
                columns = slice(k * lanes, (k + 1) * lanes)
                first = jnp.where(low, 0.0, fresh[RIM : 2 * RIM])
                last = jnp.where(low, fresh[half : half + RIM], 0.0)
                kept = jnp.concatenate([first, fresh[2 * RIM : half], last], axis=0)
                terms_ref[r * half : (r + 1) * half, columns] = kept.astype(BF16)

        next_term(k, tall, scale_ref, newer, older, shift_ref, keep)
        newer, older = older, newer
        if k % 2:
            pair = slice((k - 1) * lanes, (k + 1) * lanes)
            sums_ref[k // 2] = order_products(lanes, feature_ref[...], terms_ref[:, pair])


def store_sums(message_ref, blocks, exponent):
    scale, at = jnp.exp2(9.0 - exponent), 0
    for block in blocks:
        for row in range(0, block.shape[0], 8):
            message_ref[at : at + 8, :] = block[row : row + 8] * scale
            at += 8
    message_ref[at:, :] = jnp.concatenate([exponent] * (NOTES // 8), axis=0)


def add_kernel(mine_ref, received_ref, out_ref):
    notes = mine_ref.shape[0] - NOTES
    mine, received = mine_ref[notes : notes + 8, :], received_ref[notes : notes + 8, :]
    scales = jnp.exp2(mine - 9.0), jnp.exp2(received - 9.0)
    sums = []
    for row in range(0, notes, 8):
        at = slice(row, row + 8)
        sums.append(mine_ref[at, :] * scales[0] + received_ref[at, :] * scales[1])
    if out_ref.shape[0] == notes:
        out_ref[...] = jnp.concatenate(sums, axis=0)
    else:
        store_sums(out_ref, sums, jnp.maximum(mine, received) + 1.0)


def edge_kernel(
    orders, own_ref, centre_ref, second_ref, first_ref, rim_ref, sums_ref,
    terms_ref, message_ref, even_ref, odd_ref, scale_ref, wide_ref, shift_ref,
):
    rows, cols = centre_ref.shape[0] // 3, centre_ref.shape[1]
    halo, lanes, quarter = orders - 1, own_ref.shape[1], cols // 4
    channels, total, tall = lanes // 2, rows + 2 * halo, 3 * RIM
    west, east = in_order("col", first_ref[...].astype(F32), second_ref[...].astype(F32))
    lane = iota((3 * rows, cols), 1)
    masks = jnp.where(lane < quarter, west[: 3 * rows], jnp.where(lane < 3 * quarter, centre_ref[...], east[: 3 * rows]))
    across = compact_scales(masks)
    begin = quarter - RIM
    spread_scales(across[begin : begin + tall], across[3 * quarter - 2 * RIM : 3 * quarter + RIM], scale_ref)

    low = iota((RIM, lanes), 1) < channels
    for q in range(total):
        n, upper_row = q % (total // 2), q >= total // 2
        strip = slice(3 * rows + n * RIM, 3 * rows + (n + 1) * RIM)
        before = swap_halves(west[strip]) if upper_row else west[strip]
        after = east[strip] if upper_row else swap_halves(east[strip])
        at = q * tall
        odd_ref[at : at + RIM, :] = jnp.where(low, before, own_ref[at : at + RIM, :])
        odd_ref[at + RIM : at + 2 * RIM, :] = own_ref[at + RIM : at + 2 * RIM, :]
        odd_ref[at + 2 * RIM : at + tall, :] = jnp.where(low, own_ref[at + 2 * RIM : at + tall, :], after)

    wide_ref[:, :lanes] = jnp.zeros((rows * RIM, lanes), F32)
    blocks = []
    shift_ref[...] = jnp.zeros_like(shift_ref)
    newer, older = odd_ref, even_ref
    for k in range(1, orders):
        def keep(q, fresh):
            r = q - halo
            if 0 <= r < rows:
                wide_ref[r * RIM : (r + 1) * RIM, k * lanes : (k + 1) * lanes] = fresh[RIM : 2 * RIM]

        next_term(k, tall, scale_ref, newer, older, shift_ref, keep)
        newer, older = older, newer
        if k % 2:
            pair = slice((k - 1) * lanes, (k + 1) * lanes)
            terms = wide_ref[:, pair].astype(BF16)
            terms_ref[:, pair] = terms
            blocks.append(sums_ref[k // 2] + order_products(lanes, rim_ref[...], terms))
    tiles = [jnp.abs(block[row : row + 8]) for block in blocks for row in range(0, channels, 8)]
    largest = functools.reduce(jnp.maximum, tiles)
    exponent = jnp.floor(jnp.log2(jnp.maximum(largest, 1e-30))) + 1.0
    store_sums(message_ref, blocks, exponent)


def mix_kernel(weight_ref, inner_ref, rim_ref, grad_ref, wide_ref, terms_ref):
    channels, rows, cols = grad_ref.shape
    half, lanes = cols // 2, 2 * channels
    terms_ref[...] = inner_ref[...]
    lane, sublane = iota((2 * RIM, lanes), 1), iota((2 * RIM, lanes), 0)
    first_columns = jnp.logical_and(lane < channels, sublane < RIM)
    last_columns = jnp.logical_and(lane >= channels, sublane >= RIM)
    for k in range(1, rim_ref.shape[1] // lanes):
        columns = slice(k * lanes, (k + 1) * lanes)
        rims = rim_ref[:, columns].astype(F32)
        for r in range(rows):
            twice = jnp.concatenate([rims[r * RIM : (r + 1) * RIM]] * 2, axis=0)
            for begin, chosen in ((r * half, first_columns), ((r + 1) * half - 2 * RIM, last_columns)):
                at = (slice(begin, begin + 2 * RIM), columns)
                terms_ref[at] = jnp.where(chosen, twice, inner_ref[at].astype(F32)).astype(BF16)
    low = iota((channels, cols), 1) < half
    mixed = lax.dot_general(weight_ref[...], terms_ref[...], NT, preferred_element_type=F32)
    for q in range(rows // 2):
        upper, lower = mixed[:channels, q * cols : (q + 1) * cols], mixed[channels:, q * cols : (q + 1) * cols]
        wide_ref[pl.ds(2 * q, channels, stride=rows), :] = jnp.where(low, upper, swap_halves(lower))
        wide_ref[pl.ds(2 * q + 1, channels, stride=rows), :] = jnp.where(low, swap_halves(upper), lower)
    grad_ref[...] = wide_ref[...].reshape(channels, rows, cols).astype(BF16)


def finish_kernel(divisor, mine_ref, other_ref, out_ref):
    channels = out_ref.shape[1]
    for b in range(out_ref.shape[0] // 2):
        at = slice(b * channels, (b + 1) * channels)
        block = (mine_ref[at, :] + other_ref[at, :]) / divisor
        out_ref[2 * b] = block[:, :channels]
        out_ref[2 * b + 1] = block[:, channels:]


def call(kernel, outs, scratch, cost, *args):
    return pl.pallas_call(
        kernel,
        out_shape=outs,
        in_specs=[pl.BlockSpec(memory_space=pltpu.VMEM)] * len(args),
        out_specs=jax.tree.map(lambda _: pl.BlockSpec(memory_space=pltpu.VMEM), outs),
        scratch_shapes=scratch,
        compiler_params=pltpu.CompilerParams(vmem_limit_bytes=32 * 1024 * 1024),
        cost_estimate=pl.CostEstimate(flops=cost, bytes_accessed=1 << 20, transcendentals=0),
    )(*args)


def swap(x, partner):
    places = range(lax.axis_size("row") * lax.axis_size("col"))
    return lax.ppermute(x, ("row", "col"), [(i, partner(i)) for i in places])


def exchange_cols(first, second):
    across = lax.axis_size("col")

    def after_odd(i):
        row, col = i // across, i % across
        return row * across + (((col - 1) % across ^ 1) + 1) % across

    second = swap(second, after_odd)
    return swap(first, lambda i: i ^ 1), second


def exchange_rows(first, second):
    across, down = lax.axis_size("col"), lax.axis_size("row")

    def after_odd(i):
        row, col = i // across, i % across
        return i ^ 1 if row in (0, down - 1) else (((row - 1) ^ 1) + 1) * across + col

    return swap(first, lambda i: (i // across ^ 1) * across + i % across), swap(second, after_odd)


def sum_everywhere(part, work, *args):
    across, down = lax.axis_size("col"), lax.axis_size("row")
    beside = list(range(1, across.bit_length() - 1))
    below = list(range(across.bit_length() - 1, (across * down).bit_length() - 1))
    turns = [(beside[n : n + 1], below[n : n + 1]) for n in range(max(len(beside), len(below)))]
    even = [bit for a, b in turns for bit in a + b]
    odd = [bit for a, b in turns for bit in b + a]
    for n, bits in enumerate(zip(even, odd)):
        message = lax.optimization_barrier(part.astype(jnp.float16))
        received = swap(message, lambda i: i ^ (1 << bits[i.bit_count() % 2]) ^ 1)
        if n == 0:
            _, *args = lax.optimization_barrier((message, *args))
            received, done = lax.optimization_barrier((received, work(*args)))
        rows = part.shape[0] - (NOTES if n == len(even) - 1 else 0)
        part = call(
            add_kernel, jax.ShapeDtypeStruct((rows, part.shape[1]), F32), [], 1 << 16,
            message.astype(F32), received.astype(F32),
        )
    return part, swap(part, lambda i: i ^ 1), done


def body(feature, cotangent, order_weight, pixel_mask):
    orders, channels, _ = order_weight.shape
    _, rows, cols = feature.shape
    half, lanes, halo = cols // 2, 2 * channels, orders - 1
    tall, total = half + 2 * RIM, rows + 2 * halo
    shape = jax.ShapeDtypeStruct
    wide = pltpu.VMEM((channels * rows, cols), F32)
    marks = shape((2 * rows, cols), BF16)

    mask16 = call(mask_kernel, marks, [], 1 << 31, pixel_mask)
    sent = shape((halo * half + 2 * rows, lanes), BF16)
    cot_body, first, second = call(
        functools.partial(pack_kernel, halo), [shape((rows * half, lanes), BF16), sent, sent], [wide], 1 << 20,
        cotangent, mask16,
    )
    first, second = exchange_rows(first, second)
    features, rims, weights = call(
        early_kernel,
        [shape((lanes, rows * half), BF16), shape((lanes, rows * RIM), BF16), shape((lanes, orders * lanes), BF16)],
        [wide], 1 << 20, feature, order_weight,
    )
    sent = shape((-(-(3 * rows + total // 2 * RIM) // 16) * 16, lanes), BF16)
    west_first, west_second = call(
        functools.partial(strips_kernel, halo), [sent, sent], [], 1 << 16, cot_body, mask16, second, first
    )
    west_first, west_second = exchange_cols(west_first, west_second)
    buffer = pltpu.VMEM((total * tall, lanes), F32)
    small = pltpu.VMEM((total * 3 * RIM, lanes), F32)
    terms = shape((rows * half, orders * lanes), BF16)
    rim_terms = shape((rows * RIM, orders * lanes), BF16)
    inner, sums, own, centre = call(
        functools.partial(interior_kernel, orders),
        [
            terms, shape((orders // 2, channels, lanes), F32), shape((total * 3 * RIM, lanes), F32),
            shape((3 * rows, cols), F32),
        ],
        [buffer, buffer, buffer, pltpu.VMEM((total * (tall + 2 * RIM), lanes), F32)], 1 << 28, cot_body, mask16, second, first, features,
    )
    outer, message = call(
        functools.partial(edge_kernel, orders), [rim_terms, shape((orders // 2 * channels + NOTES, lanes), F32)],
        [small, small, small, pltpu.VMEM(rim_terms.shape, F32), pltpu.VMEM((total * 5 * RIM, lanes), F32)], 1 << 26,
        own, centre, west_second, west_first, rims, sums,
    )
    mix = functools.partial(
        call, mix_kernel, shape((channels, rows, cols), BF16), [wide, pltpu.VMEM(terms.shape, BF16)], 1 << 20
    )
    mine, other, grad_feature = sum_everywhere(message, mix, weights, inner, outer)
    pixel_count = rows * cols * lax.axis_size("row") * lax.axis_size("col")
    grad_order = call(
        functools.partial(finish_kernel, math.sqrt(pixel_count)),
        shape((orders, channels, channels), F32), [], 1 << 16, mine, other,
    )
    return (grad_feature, grad_order)


def solution(mesh):
    placed = (P(None, "row", "col"), P(None, "row", "col"), P(), P("row", "col"))
    return jax.shard_map(
        body, mesh=mesh, in_specs=placed, out_specs=(P(None, "row", "col"), P()), check_vma=False
    )
```

```python
import functools
import math

import jax
import jax.numpy as jnp
from jax import lax
from jax.experimental import pallas as pl
from jax.experimental.pallas import tpu as pltpu
from jax.sharding import PartitionSpec as P

RIM = 8
NOTES = 16
F32 = jnp.float32
BF16 = jnp.bfloat16
NT = (((1,), (1,)), ((), ()))


def iota(shape, dim):
    return lax.broadcasted_iota(jnp.int32, shape, dim)


def swap_halves(x):
    return pltpu.roll(x, x.shape[-1] // 2, x.ndim - 1)


def even_place(axis):
    return lax.axis_index(axis) % 2 == 0


def in_order(axis, first, second):
    even, place = even_place(axis), lax.axis_index(axis)
    before, after = jnp.where(even, second, first), jnp.where(even, first, second)
    return jnp.where(place == 0, 0.0, before), jnp.where(place == lax.axis_size(axis) - 1, 0.0, after)


def mask_kernel(mask_ref, out_ref):
    mask = mask_ref[...].astype(F32)
    out_ref[...] = jnp.concatenate([mask, jnp.zeros_like(mask)], axis=0).astype(BF16)


def pack_kernel(halo, cot_ref, mask_ref, body_ref, first_ref, second_ref, wide_ref):
    channels, rows, cols = cot_ref.shape
    half, lanes = cols // 2, 2 * channels
    wide_ref[...] = cot_ref[...].astype(F32).reshape(channels * rows, cols)
    fold = (iota((half, cols), 1) % half == iota((half, cols), 0)).astype(BF16)
    left = iota((channels, cols), 1) < half
    stacked = []
    for r in range(rows):
        row = wide_ref[pl.ds(r, channels, stride=rows), :]
        stacked += [jnp.where(left, row, 0.0), jnp.where(left, 0.0, row)]
    stacked = jnp.concatenate(stacked, axis=0).astype(BF16)
    body = lax.dot_general(fold, stacked, NT, preferred_element_type=F32)
    for r in range(rows):
        body_ref[r * half : (r + 1) * half, :] = body[:, r * lanes : (r + 1) * lanes].astype(BF16)
    south, count = even_place("row"), halo * half
    for out_ref, lower in ((first_ref, south), (second_ref, jnp.logical_not(south))):
        start = pl.multiple_of(jnp.where(lower, rows * half - count, 0), half)
        out_ref[:count, :] = body_ref[pl.ds(start, count), :]
        out_ref[count:, :] = mask_ref[...]


def early_kernel(feature_ref, weight_ref, feature_out_ref, rim_out_ref, weight_out_ref, wide_ref):
    channels, rows, cols = feature_ref.shape
    lanes = 2 * channels
    wide_ref[...] = feature_ref[...].astype(F32).reshape(channels * rows, cols)
    left = iota((channels, cols), 1) < cols // 2
    for q in range(rows // 2):
        even = wide_ref[pl.ds(2 * q, channels, stride=rows), :]
        odd = wide_ref[pl.ds(2 * q + 1, channels, stride=rows), :]
        at = slice(q * cols, (q + 1) * cols)
        feature_out_ref[:channels, at] = jnp.where(left, even, swap_halves(odd)).astype(BF16)
        feature_out_ref[channels:, at] = jnp.where(left, swap_halves(even), odd).astype(BF16)
    half, shape = cols // 2, (rows * cols // 2, rows * RIM)
    pixel, target = iota(shape, 0), iota(shape, 1)
    here = target // RIM * half + target % RIM
    sides = [
        jnp.dot(feature_out_ref[...], (pixel == here + skip).astype(BF16), preferred_element_type=F32)
        for skip in (0, half - RIM)
    ]
    rim_out_ref[:channels, :] = sides[0][:channels].astype(BF16)
    rim_out_ref[channels:, :] = sides[1][channels:].astype(BF16)
    for k in range(weight_ref.shape[0]):
        weight = weight_ref[k].astype(F32) * (-1.0) ** k
        blank = jnp.zeros_like(weight)
        at = slice(k * lanes, (k + 1) * lanes)
        weight_out_ref[:channels, at] = jnp.concatenate([weight, blank], axis=1).astype(BF16)
        weight_out_ref[channels:, at] = jnp.concatenate([blank, weight], axis=1).astype(BF16)


def row_pieces(halo, half, body_ref, first_ref, second_ref, begin, size):
    rows = body_ref.shape[0] // half

    def piece(ref, r):
        return ref[r * half + begin : r * half + begin + size, :].astype(F32)

    received = [in_order("row", piece(first_ref, r), piece(second_ref, r)) for r in range(halo)]
    return [north for north, _ in received] + [piece(body_ref, r) for r in range(rows)] + [south for _, south in received]


def all_masks(halo, half, mask_ref, first_ref, second_ref):
    rows, begin = mask_ref.shape[0] // 2, halo * half
    north, south = in_order("row", first_ref[begin:, :].astype(F32), second_ref[begin:, :].astype(F32))
    return jnp.concatenate([north[:rows], mask_ref[...].astype(F32)[:rows], south[:rows]], axis=0)


def edge_lanes(masks):
    cols = masks.shape[1]
    return pltpu.roll(masks, cols // 4, 1), pltpu.roll(masks, cols - cols // 4, 1)


def strips_kernel(halo, body_ref, mask_ref, second_ref, first_ref, to_first_ref, to_second_ref):
    rows = mask_ref.shape[0] // 2
    half = body_ref.shape[0] // rows
    total = rows + 2 * halo
    marks = 3 * rows
    masks = all_masks(halo, half, mask_ref, first_ref, second_ref)
    ahead, behind = edge_lanes(masks)
    leading = row_pieces(halo, half, body_ref, first_ref, second_ref, 0, 2 * RIM)
    trailing = row_pieces(halo, half, body_ref, first_ref, second_ref, half - 2 * RIM, 2 * RIM)
    low = iota((RIM, body_ref.shape[1]), 1) < body_ref.shape[1] // 2
    west, east = [], []
    for n in range(total // 2):
        west.append(jnp.where(low, leading[n][:RIM], swap_halves(leading[n + total // 2][:RIM])))
        east.append(jnp.where(low, swap_halves(trailing[n][RIM:]), trailing[n + total // 2][RIM:]))
    spare = to_first_ref.shape[0] - total // 2 * RIM - marks
    blank = [jnp.zeros((spare, body_ref.shape[1]), F32)] if spare else []
    west, east = (jnp.concatenate([marks_sent, *x] + blank, axis=0) for marks_sent, x in ((behind, west), (ahead, east)))
    even = even_place("col")
    to_first_ref[...] = jnp.where(even, east, west).astype(BF16)
    to_second_ref[...] = jnp.where(even, west, east).astype(BF16)


def compact_scales(mask):
    rows, cols = mask.shape
    column = mask + pltpu.roll(mask, 1, 0) + pltpu.roll(mask, rows - 1, 0)
    degree = mask * (column + pltpu.roll(column, 1, 1) + pltpu.roll(column, cols - 1, 1) - mask)
    return jnp.transpose(mask * lax.rsqrt(jnp.maximum(0.5 * degree, 0.5)), (1, 0))


def spread_scales(left, right, scale_ref):
    (tall, marks), lanes = left.shape, scale_ref.shape[1]
    total = scale_ref.shape[0] // tall
    spare = jnp.zeros((tall, lanes // 2 - marks), F32)
    both = jnp.concatenate([left, spare, right, spare], axis=1)
    lane = iota((tall, lanes), 1)
    start = jnp.where(lane < lanes // 2, 0, lanes // 2) + (marks - total) // 2
    for q in range(total):
        picked = jnp.take_along_axis(both, start + q, axis=1, mode="promise_in_bounds")
        scale_ref[q * tall : (q + 1) * tall, :] = picked


def next_term(k, tall, scale_ref, newer_ref, older_ref, shift_ref, visit):
    total = scale_ref.shape[0] // tall

    def at(q):
        return slice(q * tall, (q + 1) * tall)

    def weighted(q):
        return scale_ref[at(q), :] * newer_ref[at(q), :]

    above, here = weighted(k - 1), weighted(k)
    for q in range(k, total - k):
        below = weighted(q + 1)
        beside = above + below
        column = beside + here
        begin = q * (tall + 2 * RIM) + RIM
        shift_ref[begin : begin + tall, :] = column
        nearby = beside + shift_ref[begin - 1 : begin - 1 + tall, :] + shift_ref[begin + 1 : begin + 1 + tall, :]
        fresh = scale_ref[at(q), :] * nearby
        fresh = 0.5 * fresh if k == 1 else fresh - older_ref[at(q), :]
        older_ref[at(q), :] = fresh
        visit(q, fresh)
        above, here = here, below


def order_products(lanes, feature, terms):
    channels = lanes // 2
    product = jnp.dot(feature, terms, preferred_element_type=F32)
    near, far = product[:channels], product[channels:]
    even = near[:, :lanes] + swap_halves(far[:, :lanes])
    odd = swap_halves(near[:, lanes:]) + far[:, lanes:]
    return jnp.where(iota((channels, lanes), 1) < channels, even, -odd)


def interior_kernel(
    orders, body_ref, mask_ref, second_ref, first_ref, feature_ref, terms_ref, sums_ref, own_ref, centre_ref, even_ref, odd_ref, scale_ref, shift_ref
):
    rows, cols = mask_ref.shape[0] // 2, mask_ref.shape[1]
    half, halo, lanes = cols // 2, orders - 1, body_ref.shape[1]
    tall = half + 2 * RIM
    masks = all_masks(halo, half, mask_ref, first_ref, second_ref)
    ahead, behind = edge_lanes(masks)
    centre_ref[...] = jnp.where(iota(masks.shape, 1) < half, ahead, behind)
    across = compact_scales(masks)
    rim = jnp.zeros((RIM, across.shape[1]), F32)
    left = jnp.concatenate([rim, across[: half + RIM]], axis=0)
    right = jnp.concatenate([across[half - RIM :], rim], axis=0)
    spread_scales(left, right, scale_ref)
    low = iota((RIM, lanes), 1) < lanes // 2
    for q, middle in enumerate(row_pieces(halo, half, body_ref, first_ref, second_ref, 0, half)):
        at = q * tall
        odd_ref[at : at + RIM, :] = jnp.where(low, 0.0, swap_halves(middle[half - RIM :]))
        odd_ref[at + RIM : at + RIM + half, :] = middle
        odd_ref[at + RIM + half : at + tall, :] = jnp.where(low, swap_halves(middle[:RIM]), 0.0)
        at = q * 3 * RIM
        tail = half - 2 * RIM
        own_ref[at : at + RIM, :] = jnp.where(low, 0.0, middle[tail : tail + RIM])
        own_ref[at + RIM : at + 2 * RIM, :] = jnp.where(low, middle[:RIM], middle[tail + RIM :])
        own_ref[at + 2 * RIM : at + 3 * RIM, :] = jnp.where(low, middle[RIM : 2 * RIM], 0.0)
    terms_ref[:, :lanes] = body_ref[...]
    shift_ref[...] = jnp.zeros_like(shift_ref)
    newer, older = odd_ref, even_ref
    for k in range(1, orders):
        def keep(q, fresh):
            r = q - halo
            if 0 <= r < rows:
                columns = slice(k * lanes, (k + 1) * lanes)
                first = jnp.where(low, 0.0, fresh[RIM : 2 * RIM])
                last = jnp.where(low, fresh[half : half + RIM], 0.0)
                kept = jnp.concatenate([first, fresh[2 * RIM : half], last], axis=0)
                terms_ref[r * half : (r + 1) * half, columns] = kept.astype(BF16)

        next_term(k, tall, scale_ref, newer, older, shift_ref, keep)
        newer, older = older, newer
        if k % 2:
            pair = slice((k - 1) * lanes, (k + 1) * lanes)
            sums_ref[k // 2] = order_products(lanes, feature_ref[...], terms_ref[:, pair])


def store_sums(message_ref, blocks, exponent):
    scale, at = jnp.exp2(9.0 - exponent), 0
    for block in blocks:
        for row in range(0, block.shape[0], 8):
            message_ref[at : at + 8, :] = block[row : row + 8] * scale
            at += 8
    message_ref[at:, :] = jnp.concatenate([exponent] * (NOTES // 8), axis=0)


def add_kernel(mine_ref, received_ref, out_ref):
    notes = mine_ref.shape[0] - NOTES
    mine, received = mine_ref[notes : notes + 8, :], received_ref[notes : notes + 8, :]
    scales = jnp.exp2(mine - 9.0), jnp.exp2(received - 9.0)
    sums = []
    for row in range(0, notes, 8):
        at = slice(row, row + 8)
        sums.append(mine_ref[at, :] * scales[0] + received_ref[at, :] * scales[1])
    if out_ref.shape[0] == notes:
        out_ref[...] = jnp.concatenate(sums, axis=0)
    else:
        store_sums(out_ref, sums, jnp.maximum(mine, received) + 1.0)


def edge_kernel(
    orders, own_ref, centre_ref, second_ref, first_ref, rim_ref, sums_ref,
    terms_ref, message_ref, even_ref, odd_ref, scale_ref, wide_ref, shift_ref,
):
    rows, cols = centre_ref.shape[0] // 3, centre_ref.shape[1]
    halo, lanes, quarter = orders - 1, own_ref.shape[1], cols // 4
    channels, total, tall = lanes // 2, rows + 2 * halo, 3 * RIM
    west, east = in_order("col", first_ref[...].astype(F32), second_ref[...].astype(F32))
    lane = iota((3 * rows, cols), 1)
    masks = jnp.where(lane < quarter, west[: 3 * rows], jnp.where(lane < 3 * quarter, centre_ref[...], east[: 3 * rows]))
    across = compact_scales(masks)
    begin = quarter - RIM
    spread_scales(across[begin : begin + tall], across[3 * quarter - 2 * RIM : 3 * quarter + RIM], scale_ref)

    low = iota((RIM, lanes), 1) < channels
    for q in range(total):
        n, upper_row = q % (total // 2), q >= total // 2
        strip = slice(3 * rows + n * RIM, 3 * rows + (n + 1) * RIM)
        before = swap_halves(west[strip]) if upper_row else west[strip]
        after = east[strip] if upper_row else swap_halves(east[strip])
        at = q * tall
        odd_ref[at : at + RIM, :] = jnp.where(low, before, own_ref[at : at + RIM, :])
        odd_ref[at + RIM : at + 2 * RIM, :] = own_ref[at + RIM : at + 2 * RIM, :]
        odd_ref[at + 2 * RIM : at + tall, :] = jnp.where(low, own_ref[at + 2 * RIM : at + tall, :], after)

    wide_ref[:, :lanes] = jnp.zeros((rows * RIM, lanes), F32)
    blocks = []
    shift_ref[...] = jnp.zeros_like(shift_ref)
    newer, older = odd_ref, even_ref
    for k in range(1, orders):
        def keep(q, fresh):
            r = q - halo
            if 0 <= r < rows:
                wide_ref[r * RIM : (r + 1) * RIM, k * lanes : (k + 1) * lanes] = fresh[RIM : 2 * RIM]

        next_term(k, tall, scale_ref, newer, older, shift_ref, keep)
        newer, older = older, newer
        if k % 2:
            pair = slice((k - 1) * lanes, (k + 1) * lanes)
            terms = wide_ref[:, pair].astype(BF16)
            terms_ref[:, pair] = terms
            blocks.append(sums_ref[k // 2] + order_products(lanes, rim_ref[...], terms))
    tiles = [jnp.abs(block[row : row + 8]) for block in blocks for row in range(0, channels, 8)]
    largest = functools.reduce(jnp.maximum, tiles)
    exponent = jnp.floor(jnp.log2(jnp.maximum(largest, 1e-30))) + 1.0
    store_sums(message_ref, blocks, exponent)


def mix_kernel(weight_ref, inner_ref, rim_ref, grad_ref, wide_ref, terms_ref):
    channels, rows, cols = grad_ref.shape
    half, lanes = cols // 2, 2 * channels
    terms_ref[...] = inner_ref[...]
    lane, sublane = iota((2 * RIM, lanes), 1), iota((2 * RIM, lanes), 0)
    first_columns = jnp.logical_and(lane < channels, sublane < RIM)
    last_columns = jnp.logical_and(lane >= channels, sublane >= RIM)
    for k in range(1, rim_ref.shape[1] // lanes):
        columns = slice(k * lanes, (k + 1) * lanes)
        rims = rim_ref[:, columns].astype(F32)
        for r in range(rows):
            twice = jnp.concatenate([rims[r * RIM : (r + 1) * RIM]] * 2, axis=0)
            for begin, chosen in ((r * half, first_columns), ((r + 1) * half - 2 * RIM, last_columns)):
                at = (slice(begin, begin + 2 * RIM), columns)
                terms_ref[at] = jnp.where(chosen, twice, inner_ref[at].astype(F32)).astype(BF16)
    low = iota((channels, cols), 1) < half
    mixed = lax.dot_general(weight_ref[...], terms_ref[...], NT, preferred_element_type=F32)
    for q in range(rows // 2):
        upper, lower = mixed[:channels, q * cols : (q + 1) * cols], mixed[channels:, q * cols : (q + 1) * cols]
        wide_ref[pl.ds(2 * q, channels, stride=rows), :] = jnp.where(low, upper, swap_halves(lower))
        wide_ref[pl.ds(2 * q + 1, channels, stride=rows), :] = jnp.where(low, swap_halves(upper), lower)
    grad_ref[...] = wide_ref[...].reshape(channels, rows, cols).astype(BF16)


def finish_kernel(divisor, mine_ref, other_ref, out_ref):
    channels = out_ref.shape[1]
    for b in range(out_ref.shape[0] // 2):
        at = slice(b * channels, (b + 1) * channels)
        block = (mine_ref[at, :] + other_ref[at, :]) / divisor
        out_ref[2 * b] = block[:, :channels]
        out_ref[2 * b + 1] = block[:, channels:]


def call(kernel, outs, scratch, cost, *args):
    return pl.pallas_call(
        kernel,
        out_shape=outs,
        in_specs=[pl.BlockSpec(memory_space=pltpu.VMEM)] * len(args),
        out_specs=jax.tree.map(lambda _: pl.BlockSpec(memory_space=pltpu.VMEM), outs),
        scratch_shapes=scratch,
        compiler_params=pltpu.CompilerParams(vmem_limit_bytes=32 * 1024 * 1024),
        cost_estimate=pl.CostEstimate(flops=cost, bytes_accessed=1 << 20, transcendentals=0),
    )(*args)


def swap(x, partner):
    places = range(lax.axis_size("row") * lax.axis_size("col"))
    return lax.ppermute(x, ("row", "col"), [(i, partner(i)) for i in places])


def exchange_cols(first, second):
    across = lax.axis_size("col")

    def after_odd(i):
        row, col = i // across, i % across
        return row * across + (((col - 1) % across ^ 1) + 1) % across

    second = swap(second, after_odd)
    return swap(first, lambda i: i ^ 1), second


def exchange_rows(first, second):
    across, down = lax.axis_size("col"), lax.axis_size("row")

    def after_odd(i):
        row, col = i // across, i % across
        return i ^ 1 if row in (0, down - 1) else (((row - 1) ^ 1) + 1) * across + col

    return swap(first, lambda i: (i // across ^ 1) * across + i % across), swap(second, after_odd)


def sum_everywhere(part, work, *args):
    across, down = lax.axis_size("col"), lax.axis_size("row")
    beside = list(range(1, across.bit_length() - 1))
    below = list(range(across.bit_length() - 1, (across * down).bit_length() - 1))
    even, odd = beside + below, beside[::-1] + below[::-1]
    for n, bits in enumerate(zip(even, odd)):
        message = lax.optimization_barrier(part.astype(jnp.float16))
        received = swap(message, lambda i: i ^ (1 << bits[i.bit_count() % 2]) ^ 1)
        if n == 0:
            _, *args = lax.optimization_barrier((message, *args))
            received, done = lax.optimization_barrier((received, work(*args)))
        rows = part.shape[0] - (NOTES if n == len(even) - 1 else 0)
        part = call(
            add_kernel, jax.ShapeDtypeStruct((rows, part.shape[1]), F32), [], 1 << 16,
            message.astype(F32), received.astype(F32),
        )
    return part, swap(part, lambda i: i ^ 1), done


def body(feature, cotangent, order_weight, pixel_mask):
    orders, channels, _ = order_weight.shape
    _, rows, cols = feature.shape
    half, lanes, halo = cols // 2, 2 * channels, orders - 1
    tall, total = half + 2 * RIM, rows + 2 * halo
    shape = jax.ShapeDtypeStruct
    wide = pltpu.VMEM((channels * rows, cols), F32)
    marks = shape((2 * rows, cols), BF16)

    mask16 = call(mask_kernel, marks, [], 1 << 31, pixel_mask)
    sent = shape((halo * half + 2 * rows, lanes), BF16)
    cot_body, first, second = call(
        functools.partial(pack_kernel, halo), [shape((rows * half, lanes), BF16), sent, sent], [wide], 1 << 20,
        cotangent, mask16,
    )
    first, second = exchange_rows(first, second)
    features, rims, weights = call(
        early_kernel,
        [shape((lanes, rows * half), BF16), shape((lanes, rows * RIM), BF16), shape((lanes, orders * lanes), BF16)],
        [wide], 1 << 20, feature, order_weight,
    )
    sent = shape((-(-(3 * rows + total // 2 * RIM) // 16) * 16, lanes), BF16)
    west_first, west_second = call(
        functools.partial(strips_kernel, halo), [sent, sent], [], 1 << 16, cot_body, mask16, second, first
    )
    west_first, west_second = exchange_cols(west_first, west_second)
    buffer = pltpu.VMEM((total * tall, lanes), F32)
    small = pltpu.VMEM((total * 3 * RIM, lanes), F32)
    terms = shape((rows * half, orders * lanes), BF16)
    rim_terms = shape((rows * RIM, orders * lanes), BF16)
    inner, sums, own, centre = call(
        functools.partial(interior_kernel, orders),
        [
            terms, shape((orders // 2, channels, lanes), F32), shape((total * 3 * RIM, lanes), F32),
            shape((3 * rows, cols), F32),
        ],
        [buffer, buffer, buffer, pltpu.VMEM((total * (tall + 2 * RIM), lanes), F32)], 1 << 28, cot_body, mask16, second, first, features,
    )
    outer, message = call(
        functools.partial(edge_kernel, orders), [rim_terms, shape((orders // 2 * channels + NOTES, lanes), F32)],
        [small, small, small, pltpu.VMEM(rim_terms.shape, F32), pltpu.VMEM((total * 5 * RIM, lanes), F32)], 1 << 26,
        own, centre, west_second, west_first, rims, sums,
    )
    mix = functools.partial(
        call, mix_kernel, shape((channels, rows, cols), BF16), [wide, pltpu.VMEM(terms.shape, BF16)], 1 << 20
    )
    mine, other, grad_feature = sum_everywhere(message, mix, weights, inner, outer)
    pixel_count = rows * cols * lax.axis_size("row") * lax.axis_size("col")
    grad_order = call(
        functools.partial(finish_kernel, math.sqrt(pixel_count)),
        shape((orders, channels, channels), F32), [], 1 << 16, mine, other,
    )
    return (grad_feature, grad_order)


def solution(mesh):
    placed = (P(None, "row", "col"), P(None, "row", "col"), P(), P("row", "col"))
    return jax.shard_map(
        body, mesh=mesh, in_specs=placed, out_specs=(P(None, "row", "col"), P()), check_vma=False
    )
```

```python
import functools
import math

import jax
import jax.numpy as jnp
from jax import lax
from jax.experimental import pallas as pl
from jax.experimental.pallas import tpu as pltpu
from jax.sharding import PartitionSpec as P

RIM = 8
NOTES = 16
F32 = jnp.float32
BF16 = jnp.bfloat16
NT = (((1,), (1,)), ((), ()))


def iota(shape, dim):
    return lax.broadcasted_iota(jnp.int32, shape, dim)


def swap_halves(x):
    return pltpu.roll(x, x.shape[-1] // 2, x.ndim - 1)


def even_place(axis):
    return lax.axis_index(axis) % 2 == 0


def in_order(axis, first, second):
    even, place = even_place(axis), lax.axis_index(axis)
    before, after = jnp.where(even, second, first), jnp.where(even, first, second)
    return jnp.where(place == 0, 0.0, before), jnp.where(place == lax.axis_size(axis) - 1, 0.0, after)


def mask_kernel(mask_ref, out_ref):
    mask = mask_ref[...].astype(F32)
    out_ref[...] = jnp.concatenate([mask, jnp.zeros_like(mask)], axis=0).astype(BF16)


def pack_kernel(halo, cot_ref, mask_ref, body_ref, first_ref, second_ref, wide_ref):
    channels, rows, cols = cot_ref.shape
    half, lanes = cols // 2, 2 * channels
    wide_ref[...] = cot_ref[...].astype(F32).reshape(channels * rows, cols)
    fold = (iota((half, cols), 1) % half == iota((half, cols), 0)).astype(BF16)
    left = iota((channels, cols), 1) < half
    stacked = []
    for r in range(rows):
        row = wide_ref[pl.ds(r, channels, stride=rows), :]
        stacked += [jnp.where(left, row, 0.0), jnp.where(left, 0.0, row)]
    stacked = jnp.concatenate(stacked, axis=0).astype(BF16)
    body = lax.dot_general(fold, stacked, NT, preferred_element_type=F32)
    for r in range(rows):
        body_ref[r * half : (r + 1) * half, :] = body[:, r * lanes : (r + 1) * lanes].astype(BF16)
    south, count = even_place("row"), halo * half
    for out_ref, lower in ((first_ref, south), (second_ref, jnp.logical_not(south))):
        start = pl.multiple_of(jnp.where(lower, rows * half - count, 0), half)
        out_ref[:count, :] = body_ref[pl.ds(start, count), :]
        out_ref[count:, :] = mask_ref[...]


def early_kernel(feature_ref, weight_ref, feature_out_ref, rim_out_ref, weight_out_ref, wide_ref):
    channels, rows, cols = feature_ref.shape
    lanes = 2 * channels
    wide_ref[...] = feature_ref[...].astype(F32).reshape(channels * rows, cols)
    left = iota((channels, cols), 1) < cols // 2
    for q in range(rows // 2):
        even = wide_ref[pl.ds(2 * q, channels, stride=rows), :]
        odd = wide_ref[pl.ds(2 * q + 1, channels, stride=rows), :]
        at = slice(q * cols, (q + 1) * cols)
        feature_out_ref[:channels, at] = jnp.where(left, even, swap_halves(odd)).astype(BF16)
        feature_out_ref[channels:, at] = jnp.where(left, swap_halves(even), odd).astype(BF16)
    half, shape = cols // 2, (rows * cols // 2, rows * RIM)
    pixel, target = iota(shape, 0), iota(shape, 1)
    here = target // RIM * half + target % RIM
    sides = [
        jnp.dot(feature_out_ref[...], (pixel == here + skip).astype(BF16), preferred_element_type=F32)
        for skip in (0, half - RIM)
    ]
    rim_out_ref[:channels, :] = sides[0][:channels].astype(BF16)
    rim_out_ref[channels:, :] = sides[1][channels:].astype(BF16)
    for k in range(weight_ref.shape[0]):
        weight = weight_ref[k].astype(F32) * (-1.0) ** k
        blank = jnp.zeros_like(weight)
        at = slice(k * lanes, (k + 1) * lanes)
        weight_out_ref[:channels, at] = jnp.concatenate([weight, blank], axis=1).astype(BF16)
        weight_out_ref[channels:, at] = jnp.concatenate([blank, weight], axis=1).astype(BF16)


def row_pieces(halo, half, body_ref, first_ref, second_ref, begin, size):
    rows = body_ref.shape[0] // half

    def piece(ref, r):
        return ref[r * half + begin : r * half + begin + size, :].astype(F32)

    received = [in_order("row", piece(first_ref, r), piece(second_ref, r)) for r in range(halo)]
    return [north for north, _ in received] + [piece(body_ref, r) for r in range(rows)] + [south for _, south in received]


def all_masks(halo, half, mask_ref, first_ref, second_ref):
    rows, begin = mask_ref.shape[0] // 2, halo * half
    north, south = in_order("row", first_ref[begin:, :].astype(F32), second_ref[begin:, :].astype(F32))
    return jnp.concatenate([north[:rows], mask_ref[...].astype(F32)[:rows], south[:rows]], axis=0)


def edge_lanes(masks):
    cols = masks.shape[1]
    return pltpu.roll(masks, cols // 4, 1), pltpu.roll(masks, cols - cols // 4, 1)


def strips_kernel(halo, body_ref, mask_ref, first_ref, second_ref, to_first_ref, to_second_ref):
    rows = mask_ref.shape[0] // 2
    half = body_ref.shape[0] // rows
    total = rows + 2 * halo
    marks = 3 * rows
    masks = all_masks(halo, half, mask_ref, first_ref, second_ref)
    ahead, behind = edge_lanes(masks)
    leading = row_pieces(halo, half, body_ref, first_ref, second_ref, 0, 2 * RIM)
    trailing = row_pieces(halo, half, body_ref, first_ref, second_ref, half - 2 * RIM, 2 * RIM)
    low = iota((RIM, body_ref.shape[1]), 1) < body_ref.shape[1] // 2
    west, east = [], []
    for n in range(total // 2):
        west.append(jnp.where(low, leading[n][:RIM], swap_halves(leading[n + total // 2][:RIM])))
        east.append(jnp.where(low, swap_halves(trailing[n][RIM:]), trailing[n + total // 2][RIM:]))
    spare = to_first_ref.shape[0] - total // 2 * RIM - marks
    blank = [jnp.zeros((spare, body_ref.shape[1]), F32)] if spare else []
    west, east = (jnp.concatenate([marks_sent, *x] + blank, axis=0) for marks_sent, x in ((behind, west), (ahead, east)))
    even = even_place("col")
    to_first_ref[...] = jnp.where(even, east, west).astype(BF16)
    to_second_ref[...] = jnp.where(even, west, east).astype(BF16)


def compact_scales(mask):
    rows, cols = mask.shape
    column = mask + pltpu.roll(mask, 1, 0) + pltpu.roll(mask, rows - 1, 0)
    degree = mask * (column + pltpu.roll(column, 1, 1) + pltpu.roll(column, cols - 1, 1) - mask)
    return jnp.transpose(mask * lax.rsqrt(jnp.maximum(0.5 * degree, 0.5)), (1, 0))


def spread_scales(left, right, scale_ref):
    (tall, marks), lanes = left.shape, scale_ref.shape[1]
    total = scale_ref.shape[0] // tall
    spare = jnp.zeros((tall, lanes // 2 - marks), F32)
    both = jnp.concatenate([left, spare, right, spare], axis=1)
    lane = iota((tall, lanes), 1)
    start = jnp.where(lane < lanes // 2, 0, lanes // 2) + (marks - total) // 2
    for q in range(total):
        picked = jnp.take_along_axis(both, start + q, axis=1, mode="promise_in_bounds")
        scale_ref[q * tall : (q + 1) * tall, :] = picked


def next_term(k, tall, scale_ref, newer_ref, older_ref, shift_ref, visit):
    total = scale_ref.shape[0] // tall

    def at(q):
        return slice(q * tall, (q + 1) * tall)

    def weighted(q):
        return scale_ref[at(q), :] * newer_ref[at(q), :]

    above, here = weighted(k - 1), weighted(k)
    for q in range(k, total - k):
        below = weighted(q + 1)
        beside = above + below
        column = beside + here
        begin = q * (tall + 2 * RIM) + RIM
        shift_ref[begin : begin + tall, :] = column
        nearby = beside + shift_ref[begin - 1 : begin - 1 + tall, :] + shift_ref[begin + 1 : begin + 1 + tall, :]
        fresh = scale_ref[at(q), :] * nearby
        fresh = 0.5 * fresh if k == 1 else fresh - older_ref[at(q), :]
        older_ref[at(q), :] = fresh
        visit(q, fresh)
        above, here = here, below


def order_products(lanes, feature, terms):
    channels = lanes // 2
    product = jnp.dot(feature, terms, preferred_element_type=F32)
    near, far = product[:channels], product[channels:]
    even = near[:, :lanes] + swap_halves(far[:, :lanes])
    odd = swap_halves(near[:, lanes:]) + far[:, lanes:]
    return jnp.where(iota((channels, lanes), 1) < channels, even, -odd)


def interior_kernel(
    orders, body_ref, mask_ref, first_ref, second_ref, feature_ref, terms_ref, sums_ref, own_ref, centre_ref, even_ref, odd_ref, scale_ref, shift_ref
):
    rows, cols = mask_ref.shape[0] // 2, mask_ref.shape[1]
    half, halo, lanes = cols // 2, orders - 1, body_ref.shape[1]
    tall = half + 2 * RIM
    masks = all_masks(halo, half, mask_ref, first_ref, second_ref)
    ahead, behind = edge_lanes(masks)
    centre_ref[...] = jnp.where(iota(masks.shape, 1) < half, ahead, behind)
    across = compact_scales(masks)
    rim = jnp.zeros((RIM, across.shape[1]), F32)
    left = jnp.concatenate([rim, across[: half + RIM]], axis=0)
    right = jnp.concatenate([across[half - RIM :], rim], axis=0)
    spread_scales(left, right, scale_ref)
    low = iota((RIM, lanes), 1) < lanes // 2
    for q, middle in enumerate(row_pieces(halo, half, body_ref, first_ref, second_ref, 0, half)):
        at = q * tall
        odd_ref[at : at + RIM, :] = jnp.where(low, 0.0, swap_halves(middle[half - RIM :]))
        odd_ref[at + RIM : at + RIM + half, :] = middle
        odd_ref[at + RIM + half : at + tall, :] = jnp.where(low, swap_halves(middle[:RIM]), 0.0)
        at = q * 3 * RIM
        tail = half - 2 * RIM
        own_ref[at : at + RIM, :] = jnp.where(low, 0.0, middle[tail : tail + RIM])
        own_ref[at + RIM : at + 2 * RIM, :] = jnp.where(low, middle[:RIM], middle[tail + RIM :])
        own_ref[at + 2 * RIM : at + 3 * RIM, :] = jnp.where(low, middle[RIM : 2 * RIM], 0.0)
    terms_ref[:, :lanes] = body_ref[...]
    shift_ref[...] = jnp.zeros_like(shift_ref)
    newer, older = odd_ref, even_ref
    for k in range(1, orders):
        def keep(q, fresh):
            r = q - halo
            if 0 <= r < rows:
                columns = slice(k * lanes, (k + 1) * lanes)
                first = jnp.where(low, 0.0, fresh[RIM : 2 * RIM])
                last = jnp.where(low, fresh[half : half + RIM], 0.0)
                kept = jnp.concatenate([first, fresh[2 * RIM : half], last], axis=0)
                terms_ref[r * half : (r + 1) * half, columns] = kept.astype(BF16)

        next_term(k, tall, scale_ref, newer, older, shift_ref, keep)
        newer, older = older, newer
        if k % 2:
            pair = slice((k - 1) * lanes, (k + 1) * lanes)
            sums_ref[k // 2] = order_products(lanes, feature_ref[...], terms_ref[:, pair])


def store_sums(message_ref, blocks, exponent):
    scale, at = jnp.exp2(9.0 - exponent), 0
    for block in blocks:
        for row in range(0, block.shape[0], 8):
            message_ref[at : at + 8, :] = block[row : row + 8] * scale
            at += 8
    message_ref[at:, :] = jnp.concatenate([exponent] * (NOTES // 8), axis=0)


def add_kernel(mine_ref, received_ref, out_ref):
    notes = mine_ref.shape[0] - NOTES
    mine, received = mine_ref[notes : notes + 8, :], received_ref[notes : notes + 8, :]
    scales = jnp.exp2(mine - 9.0), jnp.exp2(received - 9.0)
    sums = []
    for row in range(0, notes, 8):
        at = slice(row, row + 8)
        sums.append(mine_ref[at, :] * scales[0] + received_ref[at, :] * scales[1])
    if out_ref.shape[0] == notes:
        out_ref[...] = jnp.concatenate(sums, axis=0)
    else:
        store_sums(out_ref, sums, jnp.maximum(mine, received) + 1.0)


def edge_kernel(
    orders, own_ref, centre_ref, second_ref, first_ref, rim_ref, sums_ref,
    terms_ref, message_ref, even_ref, odd_ref, scale_ref, wide_ref, shift_ref,
):
    rows, cols = centre_ref.shape[0] // 3, centre_ref.shape[1]
    halo, lanes, quarter = orders - 1, own_ref.shape[1], cols // 4
    channels, total, tall = lanes // 2, rows + 2 * halo, 3 * RIM
    west, east = in_order("col", first_ref[...].astype(F32), second_ref[...].astype(F32))
    lane = iota((3 * rows, cols), 1)
    masks = jnp.where(lane < quarter, west[: 3 * rows], jnp.where(lane < 3 * quarter, centre_ref[...], east[: 3 * rows]))
    across = compact_scales(masks)
    begin = quarter - RIM
    spread_scales(across[begin : begin + tall], across[3 * quarter - 2 * RIM : 3 * quarter + RIM], scale_ref)

    low = iota((RIM, lanes), 1) < channels
    for q in range(total):
        n, upper_row = q % (total // 2), q >= total // 2
        strip = slice(3 * rows + n * RIM, 3 * rows + (n + 1) * RIM)
        before = swap_halves(west[strip]) if upper_row else west[strip]
        after = east[strip] if upper_row else swap_halves(east[strip])
        at = q * tall
        odd_ref[at : at + RIM, :] = jnp.where(low, before, own_ref[at : at + RIM, :])
        odd_ref[at + RIM : at + 2 * RIM, :] = own_ref[at + RIM : at + 2 * RIM, :]
        odd_ref[at + 2 * RIM : at + tall, :] = jnp.where(low, own_ref[at + 2 * RIM : at + tall, :], after)

    wide_ref[:, :lanes] = jnp.zeros((rows * RIM, lanes), F32)
    blocks = []
    shift_ref[...] = jnp.zeros_like(shift_ref)
    newer, older = odd_ref, even_ref
    for k in range(1, orders):
        def keep(q, fresh):
            r = q - halo
            if 0 <= r < rows:
                wide_ref[r * RIM : (r + 1) * RIM, k * lanes : (k + 1) * lanes] = fresh[RIM : 2 * RIM]

        next_term(k, tall, scale_ref, newer, older, shift_ref, keep)
        newer, older = older, newer
        if k % 2:
            pair = slice((k - 1) * lanes, (k + 1) * lanes)
            terms = wide_ref[:, pair].astype(BF16)
            terms_ref[:, pair] = terms
            blocks.append(sums_ref[k // 2] + order_products(lanes, rim_ref[...], terms))
    tiles = [jnp.abs(block[row : row + 8]) for block in blocks for row in range(0, channels, 8)]
    largest = functools.reduce(jnp.maximum, tiles)
    exponent = jnp.floor(jnp.log2(jnp.maximum(largest, 1e-30))) + 1.0
    store_sums(message_ref, blocks, exponent)


def mix_kernel(weight_ref, inner_ref, rim_ref, grad_ref, wide_ref, terms_ref):
    channels, rows, cols = grad_ref.shape
    half, lanes = cols // 2, 2 * channels
    terms_ref[...] = inner_ref[...]
    lane, sublane = iota((2 * RIM, lanes), 1), iota((2 * RIM, lanes), 0)
    first_columns = jnp.logical_and(lane < channels, sublane < RIM)
    last_columns = jnp.logical_and(lane >= channels, sublane >= RIM)
    for k in range(1, rim_ref.shape[1] // lanes):
        columns = slice(k * lanes, (k + 1) * lanes)
        rims = rim_ref[:, columns].astype(F32)
        for r in range(rows):
            twice = jnp.concatenate([rims[r * RIM : (r + 1) * RIM]] * 2, axis=0)
            for begin, chosen in ((r * half, first_columns), ((r + 1) * half - 2 * RIM, last_columns)):
                at = (slice(begin, begin + 2 * RIM), columns)
                terms_ref[at] = jnp.where(chosen, twice, inner_ref[at].astype(F32)).astype(BF16)
    low = iota((channels, cols), 1) < half
    mixed = lax.dot_general(weight_ref[...], terms_ref[...], NT, preferred_element_type=F32)
    for q in range(rows // 2):
        upper, lower = mixed[:channels, q * cols : (q + 1) * cols], mixed[channels:, q * cols : (q + 1) * cols]
        wide_ref[pl.ds(2 * q, channels, stride=rows), :] = jnp.where(low, upper, swap_halves(lower))
        wide_ref[pl.ds(2 * q + 1, channels, stride=rows), :] = jnp.where(low, swap_halves(upper), lower)
    grad_ref[...] = wide_ref[...].reshape(channels, rows, cols).astype(BF16)


def finish_kernel(divisor, mine_ref, other_ref, out_ref):
    channels = out_ref.shape[1]
    for b in range(out_ref.shape[0] // 2):
        at = slice(b * channels, (b + 1) * channels)
        block = (mine_ref[at, :] + other_ref[at, :]) / divisor
        out_ref[2 * b] = block[:, :channels]
        out_ref[2 * b + 1] = block[:, channels:]


def call(kernel, outs, scratch, cost, *args):
    return pl.pallas_call(
        kernel,
        out_shape=outs,
        in_specs=[pl.BlockSpec(memory_space=pltpu.VMEM)] * len(args),
        out_specs=jax.tree.map(lambda _: pl.BlockSpec(memory_space=pltpu.VMEM), outs),
        scratch_shapes=scratch,
        compiler_params=pltpu.CompilerParams(vmem_limit_bytes=32 * 1024 * 1024),
        cost_estimate=pl.CostEstimate(flops=cost, bytes_accessed=1 << 20, transcendentals=0),
    )(*args)


def swap(x, partner):
    places = range(lax.axis_size("row") * lax.axis_size("col"))
    return lax.ppermute(x, ("row", "col"), [(i, partner(i)) for i in places])


def exchange_cols(first, second):
    across = lax.axis_size("col")

    def after_odd(i):
        row, col = i // across, i % across
        return row * across + (((col - 1) % across ^ 1) + 1) % across

    second = swap(second, after_odd)
    return swap(first, lambda i: i ^ 1), second


def exchange_rows(first, second):
    across, down = lax.axis_size("col"), lax.axis_size("row")

    def after_odd(i):
        row, col = i // across, i % across
        return i ^ 1 if row in (0, down - 1) else (((row - 1) ^ 1) + 1) * across + col

    return swap(first, lambda i: (i // across ^ 1) * across + i % across), swap(second, after_odd)


def sum_everywhere(part, work, *args):
    across, down = lax.axis_size("col"), lax.axis_size("row")
    beside = list(range(1, across.bit_length() - 1))
    below = list(range(across.bit_length() - 1, (across * down).bit_length() - 1))
    turns = [(beside[n : n + 1], below[n : n + 1]) for n in range(max(len(beside), len(below)))]
    even = [bit for a, b in turns for bit in a + b]
    odd = [bit for a, b in turns for bit in b + a]
    for n, bits in enumerate(zip(even, odd)):
        message = lax.optimization_barrier(part.astype(jnp.float16))
        received = swap(message, lambda i: i ^ (1 << bits[i.bit_count() % 2]) ^ 1)
        if n == 0:
            _, *args = lax.optimization_barrier((message, *args))
            received, done = lax.optimization_barrier((received, work(*args)))
        rows = part.shape[0] - (NOTES if n == len(even) - 1 else 0)
        part = call(
            add_kernel, jax.ShapeDtypeStruct((rows, part.shape[1]), F32), [], 1 << 16,
            message.astype(F32), received.astype(F32),
        )
    return part, swap(part, lambda i: i ^ 1), done


def body(feature, cotangent, order_weight, pixel_mask):
    orders, channels, _ = order_weight.shape
    _, rows, cols = feature.shape
    half, lanes, halo = cols // 2, 2 * channels, orders - 1
    tall, total = half + 2 * RIM, rows + 2 * halo
    shape = jax.ShapeDtypeStruct
    wide = pltpu.VMEM((channels * rows, cols), F32)
    marks = shape((2 * rows, cols), BF16)

    mask16 = call(mask_kernel, marks, [], 1 << 31, pixel_mask)
    sent = shape((halo * half + 2 * rows, lanes), BF16)
    cot_body, first, second = call(
        functools.partial(pack_kernel, halo), [shape((rows * half, lanes), BF16), sent, sent], [wide], 1 << 20,
        cotangent, mask16,
    )
    first, second = exchange_rows(first, second)
    features, rims, weights = call(
        early_kernel,
        [shape((lanes, rows * half), BF16), shape((lanes, rows * RIM), BF16), shape((lanes, orders * lanes), BF16)],
        [wide], 1 << 20, feature, order_weight,
    )
    sent = shape((-(-(3 * rows + total // 2 * RIM) // 16) * 16, lanes), BF16)
    west_first, west_second = call(
        functools.partial(strips_kernel, halo), [sent, sent], [], 1 << 16, cot_body, mask16, first, second
    )
    west_first, west_second = exchange_cols(west_first, west_second)
    buffer = pltpu.VMEM((total * tall, lanes), F32)
    small = pltpu.VMEM((total * 3 * RIM, lanes), F32)
    terms = shape((rows * half, orders * lanes), BF16)
    rim_terms = shape((rows * RIM, orders * lanes), BF16)
    inner, sums, own, centre = call(
        functools.partial(interior_kernel, orders),
        [
            terms, shape((orders // 2, channels, lanes), F32), shape((total * 3 * RIM, lanes), F32),
            shape((3 * rows, cols), F32),
        ],
        [buffer, buffer, buffer, pltpu.VMEM((total * (tall + 2 * RIM), lanes), F32)], 1 << 28, cot_body, mask16, first, second, features,
    )
    outer, message = call(
        functools.partial(edge_kernel, orders), [rim_terms, shape((orders // 2 * channels + NOTES, lanes), F32)],
        [small, small, small, pltpu.VMEM(rim_terms.shape, F32), pltpu.VMEM((total * 5 * RIM, lanes), F32)], 1 << 26,
        own, centre, west_second, west_first, rims, sums,
    )
    mix = functools.partial(
        call, mix_kernel, shape((channels, rows, cols), BF16), [wide, pltpu.VMEM(terms.shape, BF16)], 1 << 20
    )
    mine, other, grad_feature = sum_everywhere(message, mix, weights, inner, outer)
    pixel_count = rows * cols * lax.axis_size("row") * lax.axis_size("col")
    grad_order = call(
        functools.partial(finish_kernel, math.sqrt(pixel_count)),
        shape((orders, channels, channels), F32), [], 1 << 16, mine, other,
    )
    return (grad_feature, grad_order)


def solution(mesh):
    placed = (P(None, "row", "col"), P(None, "row", "col"), P(), P("row", "col"))
    return jax.shard_map(
        body, mesh=mesh, in_specs=placed, out_specs=(P(None, "row", "col"), P()), check_vma=False
    )
```

```python
import functools
import math

import jax
import jax.numpy as jnp
from jax import lax
from jax.experimental import pallas as pl
from jax.experimental.pallas import tpu as pltpu
from jax.sharding import PartitionSpec as P

RIM = 8
NOTES = 16
F32 = jnp.float32
BF16 = jnp.bfloat16
NT = (((1,), (1,)), ((), ()))


def iota(shape, dim):
    return lax.broadcasted_iota(jnp.int32, shape, dim)


def swap_halves(x):
    return pltpu.roll(x, x.shape[-1] // 2, x.ndim - 1)


def even_place(axis):
    return lax.axis_index(axis) % 2 == 0


def in_order(axis, first, second):
    even, place = even_place(axis), lax.axis_index(axis)
    before, after = jnp.where(even, second, first), jnp.where(even, first, second)
    return jnp.where(place == 0, 0.0, before), jnp.where(place == lax.axis_size(axis) - 1, 0.0, after)


def mask_kernel(mask_ref, out_ref):
    mask = mask_ref[...].astype(F32)
    out_ref[...] = jnp.concatenate([mask, jnp.zeros_like(mask)], axis=0).astype(BF16)


def pack_kernel(halo, cot_ref, mask_ref, body_ref, first_ref, second_ref, wide_ref):
    channels, rows, cols = cot_ref.shape
    half, lanes = cols // 2, 2 * channels
    wide_ref[...] = cot_ref[...].astype(F32).reshape(channels * rows, cols)
    fold = (iota((half, cols), 1) % half == iota((half, cols), 0)).astype(BF16)
    left = iota((channels, cols), 1) < half
    stacked = []
    for r in range(rows):
        row = wide_ref[pl.ds(r, channels, stride=rows), :]
        stacked += [jnp.where(left, row, 0.0), jnp.where(left, 0.0, row)]
    stacked = jnp.concatenate(stacked, axis=0).astype(BF16)
    body = lax.dot_general(fold, stacked, NT, preferred_element_type=F32)
    for r in range(rows):
        body_ref[r * half : (r + 1) * half, :] = body[:, r * lanes : (r + 1) * lanes].astype(BF16)
    south, count = even_place("row"), halo * half
    for out_ref, lower in ((first_ref, south), (second_ref, jnp.logical_not(south))):
        start = pl.multiple_of(jnp.where(lower, rows * half - count, 0), half)
        out_ref[:count, :] = body_ref[pl.ds(start, count), :]
        out_ref[count:, :] = mask_ref[...]


def early_kernel(feature_ref, weight_ref, feature_out_ref, rim_out_ref, weight_out_ref, wide_ref):
    channels, rows, cols = feature_ref.shape
    lanes = 2 * channels
    wide_ref[...] = feature_ref[...].astype(F32).reshape(channels * rows, cols)
    left = iota((channels, cols), 1) < cols // 2
    for q in range(rows // 2):
        even = wide_ref[pl.ds(2 * q, channels, stride=rows), :]
        odd = wide_ref[pl.ds(2 * q + 1, channels, stride=rows), :]
        at = slice(q * cols, (q + 1) * cols)
        feature_out_ref[:channels, at] = jnp.where(left, even, swap_halves(odd)).astype(BF16)
        feature_out_ref[channels:, at] = jnp.where(left, swap_halves(even), odd).astype(BF16)
    half, shape = cols // 2, (rows * cols // 2, rows * RIM)
    pixel, target = iota(shape, 0), iota(shape, 1)
    here = target // RIM * half + target % RIM
    sides = [
        jnp.dot(feature_out_ref[...], (pixel == here + skip).astype(BF16), preferred_element_type=F32)
        for skip in (0, half - RIM)
    ]
    rim_out_ref[:channels, :] = sides[0][:channels].astype(BF16)
    rim_out_ref[channels:, :] = sides[1][channels:].astype(BF16)
    for k in range(weight_ref.shape[0]):
        weight = weight_ref[k].astype(F32) * (-1.0) ** k
        blank = jnp.zeros_like(weight)
        at = slice(k * lanes, (k + 1) * lanes)
        weight_out_ref[:channels, at] = jnp.concatenate([weight, blank], axis=1).astype(BF16)
        weight_out_ref[channels:, at] = jnp.concatenate([blank, weight], axis=1).astype(BF16)


def row_pieces(halo, half, body_ref, first_ref, second_ref, begin, size):
    rows = body_ref.shape[0] // half

    def piece(ref, r):
        return ref[r * half + begin : r * half + begin + size, :].astype(F32)

    received = [in_order("row", piece(first_ref, r), piece(second_ref, r)) for r in range(halo)]
    return [north for north, _ in received] + [piece(body_ref, r) for r in range(rows)] + [south for _, south in received]


def all_masks(halo, half, mask_ref, first_ref, second_ref):
    rows, begin = mask_ref.shape[0] // 2, halo * half
    north, south = in_order("row", first_ref[begin:, :].astype(F32), second_ref[begin:, :].astype(F32))
    return jnp.concatenate([north[:rows], mask_ref[...].astype(F32)[:rows], south[:rows]], axis=0)


def edge_lanes(masks):
    cols = masks.shape[1]
    return pltpu.roll(masks, cols // 4, 1), pltpu.roll(masks, cols - cols // 4, 1)


def strips_kernel(halo, body_ref, mask_ref, second_ref, first_ref, to_first_ref, to_second_ref):
    rows = mask_ref.shape[0] // 2
    half = body_ref.shape[0] // rows
    total = rows + 2 * halo
    marks = 3 * rows
    masks = all_masks(halo, half, mask_ref, first_ref, second_ref)
    ahead, behind = edge_lanes(masks)
    leading = row_pieces(halo, half, body_ref, first_ref, second_ref, 0, 2 * RIM)
    trailing = row_pieces(halo, half, body_ref, first_ref, second_ref, half - 2 * RIM, 2 * RIM)
    low = iota((RIM, body_ref.shape[1]), 1) < body_ref.shape[1] // 2
    west, east = [], []
    for n in range(total // 2):
        west.append(jnp.where(low, leading[n][:RIM], swap_halves(leading[n + total // 2][:RIM])))
        east.append(jnp.where(low, swap_halves(trailing[n][RIM:]), trailing[n + total // 2][RIM:]))
    spare = to_first_ref.shape[0] - total // 2 * RIM - marks
    blank = [jnp.zeros((spare, body_ref.shape[1]), F32)] if spare else []
    west, east = (jnp.concatenate([marks_sent, *x] + blank, axis=0) for marks_sent, x in ((behind, west), (ahead, east)))
    even = even_place("col")
    to_first_ref[...] = jnp.where(even, east, west).astype(BF16)
    to_second_ref[...] = jnp.where(even, west, east).astype(BF16)


def compact_scales(mask):
    rows, cols = mask.shape
    column = mask + pltpu.roll(mask, 1, 0) + pltpu.roll(mask, rows - 1, 0)
    degree = mask * (column + pltpu.roll(column, 1, 1) + pltpu.roll(column, cols - 1, 1) - mask)
    return jnp.transpose(mask * lax.rsqrt(jnp.maximum(0.5 * degree, 0.5)), (1, 0))


def spread_scales(left, right, scale_ref):
    (tall, marks), lanes = left.shape, scale_ref.shape[1]
    total = scale_ref.shape[0] // tall
    spare = jnp.zeros((tall, lanes // 2 - marks), F32)
    both = jnp.concatenate([left, spare, right, spare], axis=1)
    lane = iota((tall, lanes), 1)
    start = jnp.where(lane < lanes // 2, 0, lanes // 2) + (marks - total) // 2
    for q in range(total):
        picked = jnp.take_along_axis(both, start + q, axis=1, mode="promise_in_bounds")
        scale_ref[q * tall : (q + 1) * tall, :] = picked


def clear_rims(tall, shift_ref):
    whole = tall + 2 * RIM
    for begin in range(0, shift_ref.shape[0], whole):
        for at in (begin, begin + whole - RIM):
            shift_ref[at : at + RIM, :] = jnp.zeros((RIM, shift_ref.shape[1]), F32)


def next_term(k, tall, scale_ref, newer_ref, older_ref, shift_ref, visit):
    total = scale_ref.shape[0] // tall

    def at(q):
        return slice(q * tall, (q + 1) * tall)

    def weighted(q):
        return scale_ref[at(q), :] * newer_ref[at(q), :]

    above, here = weighted(k - 1), weighted(k)
    for q in range(k, total - k):
        below = weighted(q + 1)
        beside = above + below
        column = beside + here
        begin = q * (tall + 2 * RIM) + RIM
        shift_ref[begin : begin + tall, :] = column
        nearby = beside + shift_ref[begin - 1 : begin - 1 + tall, :] + shift_ref[begin + 1 : begin + 1 + tall, :]
        fresh = scale_ref[at(q), :] * nearby
        fresh = 0.5 * fresh if k == 1 else fresh - older_ref[at(q), :]
        older_ref[at(q), :] = fresh
        visit(q, fresh)
        above, here = here, below


def order_products(lanes, feature, terms):
    channels = lanes // 2
    product = jnp.dot(feature, terms, preferred_element_type=F32)
    near, far = product[:channels], product[channels:]
    even = near[:, :lanes] + swap_halves(far[:, :lanes])
    odd = swap_halves(near[:, lanes:]) + far[:, lanes:]
    return jnp.where(iota((channels, lanes), 1) < channels, even, -odd)


def interior_kernel(
    orders, body_ref, mask_ref, second_ref, first_ref, feature_ref, terms_ref, sums_ref, own_ref, centre_ref, even_ref, odd_ref, scale_ref, shift_ref
):
    rows, cols = mask_ref.shape[0] // 2, mask_ref.shape[1]
    half, halo, lanes = cols // 2, orders - 1, body_ref.shape[1]
    tall = half + 2 * RIM
    masks = all_masks(halo, half, mask_ref, first_ref, second_ref)
    ahead, behind = edge_lanes(masks)
    centre_ref[...] = jnp.where(iota(masks.shape, 1) < half, ahead, behind)
    across = compact_scales(masks)
    rim = jnp.zeros((RIM, across.shape[1]), F32)
    left = jnp.concatenate([rim, across[: half + RIM]], axis=0)
    right = jnp.concatenate([across[half - RIM :], rim], axis=0)
    spread_scales(left, right, scale_ref)
    low = iota((RIM, lanes), 1) < lanes // 2
    for q, middle in enumerate(row_pieces(halo, half, body_ref, first_ref, second_ref, 0, half)):
        at = q * tall
        odd_ref[at : at + RIM, :] = jnp.where(low, 0.0, swap_halves(middle[half - RIM :]))
        odd_ref[at + RIM : at + RIM + half, :] = middle
        odd_ref[at + RIM + half : at + tall, :] = jnp.where(low, swap_halves(middle[:RIM]), 0.0)
        at = q * 3 * RIM
        tail = half - 2 * RIM
        own_ref[at : at + RIM, :] = jnp.where(low, 0.0, middle[tail : tail + RIM])
        own_ref[at + RIM : at + 2 * RIM, :] = jnp.where(low, middle[:RIM], middle[tail + RIM :])
        own_ref[at + 2 * RIM : at + 3 * RIM, :] = jnp.where(low, middle[RIM : 2 * RIM], 0.0)
    terms_ref[:, :lanes] = body_ref[...]
    clear_rims(tall, shift_ref)
    newer, older = odd_ref, even_ref
    for k in range(1, orders):
        def keep(q, fresh):
            r = q - halo
            if 0 <= r < rows:
                columns = slice(k * lanes, (k + 1) * lanes)
                first = jnp.where(low, 0.0, fresh[RIM : 2 * RIM])
                last = jnp.where(low, fresh[half : half + RIM], 0.0)
                kept = jnp.concatenate([first, fresh[2 * RIM : half], last], axis=0)
                terms_ref[r * half : (r + 1) * half, columns] = kept.astype(BF16)

        next_term(k, tall, scale_ref, newer, older, shift_ref, keep)
        newer, older = older, newer
        if k % 2:
            pair = slice((k - 1) * lanes, (k + 1) * lanes)
            sums_ref[k // 2] = order_products(lanes, feature_ref[...], terms_ref[:, pair])


def store_sums(message_ref, blocks, exponent):
    scale, at = jnp.exp2(9.0 - exponent), 0
    for block in blocks:
        for row in range(0, block.shape[0], 8):
            message_ref[at : at + 8, :] = block[row : row + 8] * scale
            at += 8
    message_ref[at:, :] = jnp.concatenate([exponent] * (NOTES // 8), axis=0)


def decoded_sums(mine_ref, received_ref):
    notes = mine_ref.shape[0] - NOTES
    mine, received = mine_ref[notes : notes + 8, :], received_ref[notes : notes + 8, :]
    scales = jnp.exp2(mine - 9.0), jnp.exp2(received - 9.0)
    sums = []
    for row in range(0, notes, 8):
        at = slice(row, row + 8)
        sums.append(mine_ref[at, :] * scales[0] + received_ref[at, :] * scales[1])
    return sums, jnp.maximum(mine, received) + 1.0


def add_kernel(mine_ref, received_ref, out_ref):
    store_sums(out_ref, *decoded_sums(mine_ref, received_ref))


def edge_kernel(
    orders, own_ref, centre_ref, second_ref, first_ref, rim_ref, sums_ref,
    terms_ref, message_ref, even_ref, odd_ref, scale_ref, wide_ref, shift_ref,
):
    rows, cols = centre_ref.shape[0] // 3, centre_ref.shape[1]
    halo, lanes, quarter = orders - 1, own_ref.shape[1], cols // 4
    channels, total, tall = lanes // 2, rows + 2 * halo, 3 * RIM
    west, east = in_order("col", first_ref[...].astype(F32), second_ref[...].astype(F32))
    lane = iota((3 * rows, cols), 1)
    masks = jnp.where(lane < quarter, west[: 3 * rows], jnp.where(lane < 3 * quarter, centre_ref[...], east[: 3 * rows]))
    across = compact_scales(masks)
    begin = quarter - RIM
    spread_scales(across[begin : begin + tall], across[3 * quarter - 2 * RIM : 3 * quarter + RIM], scale_ref)

    low = iota((RIM, lanes), 1) < channels
    for q in range(total):
        n, upper_row = q % (total // 2), q >= total // 2
        strip = slice(3 * rows + n * RIM, 3 * rows + (n + 1) * RIM)
        before = swap_halves(west[strip]) if upper_row else west[strip]
        after = east[strip] if upper_row else swap_halves(east[strip])
        at = q * tall
        odd_ref[at : at + RIM, :] = jnp.where(low, before, own_ref[at : at + RIM, :])
        odd_ref[at + RIM : at + 2 * RIM, :] = own_ref[at + RIM : at + 2 * RIM, :]
        odd_ref[at + 2 * RIM : at + tall, :] = jnp.where(low, own_ref[at + 2 * RIM : at + tall, :], after)

    wide_ref[:, :lanes] = jnp.zeros((rows * RIM, lanes), F32)
    blocks = []
    clear_rims(tall, shift_ref)
    newer, older = odd_ref, even_ref
    for k in range(1, orders):
        def keep(q, fresh):
            r = q - halo
            if 0 <= r < rows:
                wide_ref[r * RIM : (r + 1) * RIM, k * lanes : (k + 1) * lanes] = fresh[RIM : 2 * RIM]

        next_term(k, tall, scale_ref, newer, older, shift_ref, keep)
        newer, older = older, newer
        if k % 2:
            pair = slice((k - 1) * lanes, (k + 1) * lanes)
            terms = wide_ref[:, pair].astype(BF16)
            terms_ref[:, pair] = terms
            blocks.append(sums_ref[k // 2] + order_products(lanes, rim_ref[...], terms))
    tiles = [jnp.abs(block[row : row + 8]) for block in blocks for row in range(0, channels, 8)]
    largest = functools.reduce(jnp.maximum, tiles)
    exponent = jnp.floor(jnp.log2(jnp.maximum(largest, 1e-30))) + 1.0
    store_sums(message_ref, blocks, exponent)


def mix_kernel(weight_ref, inner_ref, rim_ref, grad_ref, wide_ref, terms_ref):
    channels, rows, cols = grad_ref.shape
    half, lanes = cols // 2, 2 * channels
    terms_ref[...] = inner_ref[...]
    lane, sublane = iota((2 * RIM, lanes), 1), iota((2 * RIM, lanes), 0)
    first_columns = jnp.logical_and(lane < channels, sublane < RIM)
    last_columns = jnp.logical_and(lane >= channels, sublane >= RIM)
    for k in range(1, rim_ref.shape[1] // lanes):
        columns = slice(k * lanes, (k + 1) * lanes)
        rims = rim_ref[:, columns].astype(F32)
        for r in range(rows):
            twice = jnp.concatenate([rims[r * RIM : (r + 1) * RIM]] * 2, axis=0)
            for begin, chosen in ((r * half, first_columns), ((r + 1) * half - 2 * RIM, last_columns)):
                at = (slice(begin, begin + 2 * RIM), columns)
                terms_ref[at] = jnp.where(chosen, twice, inner_ref[at].astype(F32)).astype(BF16)
    low = iota((channels, cols), 1) < half
    mixed = lax.dot_general(weight_ref[...], terms_ref[...], NT, preferred_element_type=F32)
    for q in range(rows // 2):
        upper, lower = mixed[:channels, q * cols : (q + 1) * cols], mixed[channels:, q * cols : (q + 1) * cols]
        wide_ref[pl.ds(2 * q, channels, stride=rows), :] = jnp.where(low, upper, swap_halves(lower))
        wide_ref[pl.ds(2 * q + 1, channels, stride=rows), :] = jnp.where(low, swap_halves(upper), lower)
    grad_ref[...] = wide_ref[...].reshape(channels, rows, cols).astype(BF16)


def finish_kernel(divisor, mine_ref, other_ref, out_ref):
    channels = out_ref.shape[1]
    sums, _ = decoded_sums(mine_ref, other_ref)
    for n, block in enumerate(sums):
        b, row = n * 8 // channels, n * 8 % channels
        block = block / divisor
        out_ref[2 * b, row : row + 8, :] = block[:, :channels]
        out_ref[2 * b + 1, row : row + 8, :] = block[:, channels:]


def call(kernel, outs, scratch, cost, *args):
    return pl.pallas_call(
        kernel,
        out_shape=outs,
        in_specs=[pl.BlockSpec(memory_space=pltpu.VMEM)] * len(args),
        out_specs=jax.tree.map(lambda _: pl.BlockSpec(memory_space=pltpu.VMEM), outs),
        scratch_shapes=scratch,
        compiler_params=pltpu.CompilerParams(vmem_limit_bytes=32 * 1024 * 1024),
        cost_estimate=pl.CostEstimate(flops=cost, bytes_accessed=1 << 20, transcendentals=0),
    )(*args)


def swap(x, partner):
    places = range(lax.axis_size("row") * lax.axis_size("col"))
    return lax.ppermute(x, ("row", "col"), [(i, partner(i)) for i in places])


def exchange_cols(first, second):
    across = lax.axis_size("col")

    def after_odd(i):
        row, col = i // across, i % across
        return row * across + (((col - 1) % across ^ 1) + 1) % across

    second = swap(second, after_odd)
    return swap(first, lambda i: i ^ 1), second


def exchange_rows(first, second):
    across, down = lax.axis_size("col"), lax.axis_size("row")

    def after_odd(i):
        row, col = i // across, i % across
        return i ^ 1 if row in (0, down - 1) else (((row - 1) ^ 1) + 1) * across + col

    return swap(first, lambda i: (i // across ^ 1) * across + i % across), swap(second, after_odd)


def sum_everywhere(part, work, *args):
    across, down = lax.axis_size("col"), lax.axis_size("row")
    beside = list(range(1, across.bit_length() - 1))
    below = list(range(across.bit_length() - 1, (across * down).bit_length() - 1))
    turns = [(beside[n : n + 1], below[n : n + 1]) for n in range(max(len(beside), len(below)))]
    even = [bit for a, b in turns for bit in a + b]
    odd = [bit for a, b in turns for bit in b + a]
    for n, bits in enumerate(zip(even, odd)):
        message = lax.optimization_barrier(part.astype(jnp.float16))
        received = swap(message, lambda i: i ^ (1 << bits[i.bit_count() % 2]) ^ 1)
        if n == 0:
            _, *args = lax.optimization_barrier((message, *args))
            received, done = lax.optimization_barrier((received, work(*args)))
        part = call(
            add_kernel, jax.ShapeDtypeStruct(part.shape, F32), [], 1 << 16, message.astype(F32), received.astype(F32)
        )
    message = lax.optimization_barrier(part.astype(jnp.float16))
    return message.astype(F32), swap(message, lambda i: i ^ 1).astype(F32), done


def body(feature, cotangent, order_weight, pixel_mask):
    orders, channels, _ = order_weight.shape
    _, rows, cols = feature.shape
    half, lanes, halo = cols // 2, 2 * channels, orders - 1
    tall, total = half + 2 * RIM, rows + 2 * halo
    shape = jax.ShapeDtypeStruct
    wide = pltpu.VMEM((channels * rows, cols), F32)
    marks = shape((2 * rows, cols), BF16)

    mask16 = call(mask_kernel, marks, [], 1 << 31, pixel_mask)
    sent = shape((halo * half + 2 * rows, lanes), BF16)
    cot_body, first, second = call(
        functools.partial(pack_kernel, halo), [shape((rows * half, lanes), BF16), sent, sent], [wide], 1 << 20,
        cotangent, mask16,
    )
    first, second = exchange_rows(first, second)
    features, rims, weights = call(
        early_kernel,
        [shape((lanes, rows * half), BF16), shape((lanes, rows * RIM), BF16), shape((lanes, orders * lanes), BF16)],
        [wide], 1 << 20, feature, order_weight,
    )
    sent = shape((-(-(3 * rows + total // 2 * RIM) // 16) * 16, lanes), BF16)
    west_first, west_second = call(
        functools.partial(strips_kernel, halo), [sent, sent], [], 1 << 16, cot_body, mask16, second, first
    )
    west_first, west_second = exchange_cols(west_first, west_second)
    buffer = pltpu.VMEM((total * tall, lanes), F32)
    small = pltpu.VMEM((total * 3 * RIM, lanes), F32)
    terms = shape((rows * half, orders * lanes), BF16)
    rim_terms = shape((rows * RIM, orders * lanes), BF16)
    inner, sums, own, centre = call(
        functools.partial(interior_kernel, orders),
        [
            terms, shape((orders // 2, channels, lanes), F32), shape((total * 3 * RIM, lanes), F32),
            shape((3 * rows, cols), F32),
        ],
        [buffer, buffer, buffer, pltpu.VMEM((total * (tall + 2 * RIM), lanes), F32)], 1 << 28, cot_body, mask16, second, first, features,
    )
    outer, message = call(
        functools.partial(edge_kernel, orders), [rim_terms, shape((orders // 2 * channels + NOTES, lanes), F32)],
        [small, small, small, pltpu.VMEM(rim_terms.shape, F32), pltpu.VMEM((total * 5 * RIM, lanes), F32)], 1 << 26,
        own, centre, west_second, west_first, rims, sums,
    )
    mix = functools.partial(
        call, mix_kernel, shape((channels, rows, cols), BF16), [wide, pltpu.VMEM(terms.shape, BF16)], 1 << 20
    )
    mine, other, grad_feature = sum_everywhere(message, mix, weights, inner, outer)
    pixel_count = rows * cols * lax.axis_size("row") * lax.axis_size("col")
    grad_order = call(
        functools.partial(finish_kernel, math.sqrt(pixel_count)),
        shape((orders, channels, channels), F32), [], 1 << 16, mine, other,
    )
    return (grad_feature, grad_order)


def solution(mesh):
    placed = (P(None, "row", "col"), P(None, "row", "col"), P(), P("row", "col"))
    return jax.shard_map(
        body, mesh=mesh, in_specs=placed, out_specs=(P(None, "row", "col"), P()), check_vma=False
    )
```

```python
import functools
import math

import jax
import jax.numpy as jnp
from jax import lax
from jax.experimental import pallas as pl
from jax.experimental.pallas import tpu as pltpu
from jax.sharding import PartitionSpec as P

RIM = 8
NOTES = 16
F32 = jnp.float32
BF16 = jnp.bfloat16
NT = (((1,), (1,)), ((), ()))


def iota(shape, dim):
    return lax.broadcasted_iota(jnp.int32, shape, dim)


def swap_halves(x):
    return pltpu.roll(x, x.shape[-1] // 2, x.ndim - 1)


def even_place(axis):
    return lax.axis_index(axis) % 2 == 0


def in_order(axis, first, second):
    even, place = even_place(axis), lax.axis_index(axis)
    before, after = jnp.where(even, second, first), jnp.where(even, first, second)
    return jnp.where(place == 0, 0.0, before), jnp.where(place == lax.axis_size(axis) - 1, 0.0, after)


def mask_kernel(mask_ref, out_ref):
    mask = mask_ref[...].astype(F32)
    out_ref[...] = jnp.concatenate([mask, jnp.zeros_like(mask)], axis=0).astype(BF16)


def pack_kernel(halo, cot_ref, mask_ref, body_ref, first_ref, second_ref, wide_ref):
    channels, rows, cols = cot_ref.shape
    half, lanes = cols // 2, 2 * channels
    wide_ref[...] = cot_ref[...].astype(F32).reshape(channels * rows, cols)
    fold = (iota((half, cols), 1) % half == iota((half, cols), 0)).astype(BF16)
    left = iota((channels, cols), 1) < half
    stacked = []
    for r in range(rows):
        row = wide_ref[pl.ds(r, channels, stride=rows), :]
        stacked += [jnp.where(left, row, 0.0), jnp.where(left, 0.0, row)]
    stacked = jnp.concatenate(stacked, axis=0).astype(BF16)
    body = lax.dot_general(fold, stacked, NT, preferred_element_type=F32)
    for r in range(rows):
        body_ref[r * half : (r + 1) * half, :] = body[:, r * lanes : (r + 1) * lanes].astype(BF16)
    south, count = even_place("row"), halo * half
    for out_ref, lower in ((first_ref, south), (second_ref, jnp.logical_not(south))):
        start = pl.multiple_of(jnp.where(lower, rows * half - count, 0), half)
        out_ref[:count, :] = body_ref[pl.ds(start, count), :]
        out_ref[count:, :] = mask_ref[...]


def early_kernel(feature_ref, weight_ref, feature_out_ref, rim_out_ref, weight_out_ref, wide_ref):
    channels, rows, cols = feature_ref.shape
    lanes = 2 * channels
    wide_ref[...] = feature_ref[...].astype(F32).reshape(channels * rows, cols)
    left = iota((channels, cols), 1) < cols // 2
    for q in range(rows // 2):
        even = wide_ref[pl.ds(2 * q, channels, stride=rows), :]
        odd = wide_ref[pl.ds(2 * q + 1, channels, stride=rows), :]
        at = slice(q * cols, (q + 1) * cols)
        feature_out_ref[:channels, at] = jnp.where(left, even, swap_halves(odd)).astype(BF16)
        feature_out_ref[channels:, at] = jnp.where(left, swap_halves(even), odd).astype(BF16)
    half, shape = cols // 2, (rows * cols // 2, rows * RIM)
    pixel, target = iota(shape, 0), iota(shape, 1)
    here = target // RIM * half + target % RIM
    sides = [
        jnp.dot(feature_out_ref[...], (pixel == here + skip).astype(BF16), preferred_element_type=F32)
        for skip in (0, half - RIM)
    ]
    rim_out_ref[:channels, :] = sides[0][:channels].astype(BF16)
    rim_out_ref[channels:, :] = sides[1][channels:].astype(BF16)
    for k in range(weight_ref.shape[0]):
        weight = weight_ref[k].astype(F32) * (-1.0) ** k
        blank = jnp.zeros_like(weight)
        at = slice(k * lanes, (k + 1) * lanes)
        weight_out_ref[:channels, at] = jnp.concatenate([weight, blank], axis=1).astype(BF16)
        weight_out_ref[channels:, at] = jnp.concatenate([blank, weight], axis=1).astype(BF16)


def row_pieces(halo, half, body_ref, first_ref, second_ref, begin, size):
    rows = body_ref.shape[0] // half

    def piece(ref, r):
        return ref[r * half + begin : r * half + begin + size, :].astype(F32)

    received = [in_order("row", piece(first_ref, r), piece(second_ref, r)) for r in range(halo)]
    return [north for north, _ in received] + [piece(body_ref, r) for r in range(rows)] + [south for _, south in received]


def all_masks(halo, half, mask_ref, first_ref, second_ref):
    rows, begin = mask_ref.shape[0] // 2, halo * half
    north, south = in_order("row", first_ref[begin:, :].astype(F32), second_ref[begin:, :].astype(F32))
    return jnp.concatenate([north[:rows], mask_ref[...].astype(F32)[:rows], south[:rows]], axis=0)


def edge_lanes(masks):
    cols = masks.shape[1]
    return pltpu.roll(masks, cols // 4, 1), pltpu.roll(masks, cols - cols // 4, 1)


def strips_kernel(halo, body_ref, mask_ref, second_ref, first_ref, to_first_ref, to_second_ref):
    rows = mask_ref.shape[0] // 2
    half = body_ref.shape[0] // rows
    total = rows + 2 * halo
    marks = 3 * rows
    masks = all_masks(halo, half, mask_ref, first_ref, second_ref)
    ahead, behind = edge_lanes(masks)
    leading = row_pieces(halo, half, body_ref, first_ref, second_ref, 0, 2 * RIM)
    trailing = row_pieces(halo, half, body_ref, first_ref, second_ref, half - 2 * RIM, 2 * RIM)
    low = iota((RIM, body_ref.shape[1]), 1) < body_ref.shape[1] // 2
    west, east = [], []
    for n in range(total // 2):
        west.append(jnp.where(low, leading[n][:RIM], swap_halves(leading[n + total // 2][:RIM])))
        east.append(jnp.where(low, swap_halves(trailing[n][RIM:]), trailing[n + total // 2][RIM:]))
    spare = to_first_ref.shape[0] - total // 2 * RIM - marks
    blank = [jnp.zeros((spare, body_ref.shape[1]), F32)] if spare else []
    west, east = (jnp.concatenate([marks_sent, *x] + blank, axis=0) for marks_sent, x in ((behind, west), (ahead, east)))
    even = even_place("col")
    to_first_ref[...] = jnp.where(even, east, west).astype(BF16)
    to_second_ref[...] = jnp.where(even, west, east).astype(BF16)


def compact_scales(mask):
    rows, cols = mask.shape
    column = mask + pltpu.roll(mask, 1, 0) + pltpu.roll(mask, rows - 1, 0)
    degree = mask * (column + pltpu.roll(column, 1, 1) + pltpu.roll(column, cols - 1, 1) - mask)
    return jnp.transpose(mask * lax.rsqrt(jnp.maximum(0.5 * degree, 0.5)), (1, 0))


def spread_scales(left, right, scale_ref):
    (tall, marks), lanes = left.shape, scale_ref.shape[1]
    total = scale_ref.shape[0] // tall
    spare = jnp.zeros((tall, lanes // 2 - marks), F32)
    both = jnp.concatenate([left, spare, right, spare], axis=1)
    lane = iota((tall, lanes), 1)
    start = jnp.where(lane < lanes // 2, 0, lanes // 2) + (marks - total) // 2
    for q in range(total):
        picked = jnp.take_along_axis(both, start + q, axis=1, mode="promise_in_bounds")
        scale_ref[q * tall : (q + 1) * tall, :] = picked


def clear_rims(tall, shift_ref):
    whole = tall + 2 * RIM
    for begin in range(0, shift_ref.shape[0], whole):
        for at in (begin, begin + whole - RIM):
            shift_ref[at : at + RIM, :] = jnp.zeros((RIM, shift_ref.shape[1]), F32)


def next_term(k, tall, scale_ref, newer_ref, older_ref, shift_ref, visit):
    total = scale_ref.shape[0] // tall

    def at(q):
        return slice(q * tall, (q + 1) * tall)

    def weighted(q):
        return scale_ref[at(q), :] * newer_ref[at(q), :]

    above, here = weighted(k - 1), weighted(k)
    for q in range(k, total - k):
        below = weighted(q + 1)
        beside = above + below
        column = beside + here
        begin = q * (tall + 2 * RIM) + RIM
        shift_ref[begin : begin + tall, :] = column
        nearby = beside + shift_ref[begin - 1 : begin - 1 + tall, :] + shift_ref[begin + 1 : begin + 1 + tall, :]
        fresh = scale_ref[at(q), :] * nearby
        fresh = 0.5 * fresh if k == 1 else fresh - older_ref[at(q), :]
        older_ref[at(q), :] = fresh
        visit(q, fresh)
        above, here = here, below


def order_products(lanes, feature, terms):
    channels = lanes // 2
    product = jnp.dot(feature, terms, preferred_element_type=F32)
    near, far = product[:channels], product[channels:]
    even = near[:, :lanes] + swap_halves(far[:, :lanes])
    odd = swap_halves(near[:, lanes:]) + far[:, lanes:]
    return jnp.where(iota((channels, lanes), 1) < channels, even, -odd)


def interior_kernel(
    orders, body_ref, mask_ref, second_ref, first_ref, feature_ref, terms_ref, sums_ref, own_ref, centre_ref, even_ref, odd_ref, scale_ref, shift_ref
):
    rows, cols = mask_ref.shape[0] // 2, mask_ref.shape[1]
    half, halo, lanes = cols // 2, orders - 1, body_ref.shape[1]
    tall = half + 2 * RIM
    masks = all_masks(halo, half, mask_ref, first_ref, second_ref)
    ahead, behind = edge_lanes(masks)
    centre_ref[...] = jnp.where(iota(masks.shape, 1) < half, ahead, behind)
    across = compact_scales(masks)
    rim = jnp.zeros((RIM, across.shape[1]), F32)
    left = jnp.concatenate([rim, across[: half + RIM]], axis=0)
    right = jnp.concatenate([across[half - RIM :], rim], axis=0)
    spread_scales(left, right, scale_ref)
    low = iota((RIM, lanes), 1) < lanes // 2
    for q, middle in enumerate(row_pieces(halo, half, body_ref, first_ref, second_ref, 0, half)):
        at = q * tall
        odd_ref[at : at + RIM, :] = jnp.where(low, 0.0, swap_halves(middle[half - RIM :]))
        odd_ref[at + RIM : at + RIM + half, :] = middle
        odd_ref[at + RIM + half : at + tall, :] = jnp.where(low, swap_halves(middle[:RIM]), 0.0)
        at = q * 3 * RIM
        tail = half - 2 * RIM
        own_ref[at : at + RIM, :] = jnp.where(low, 0.0, middle[tail : tail + RIM])
        own_ref[at + RIM : at + 2 * RIM, :] = jnp.where(low, middle[:RIM], middle[tail + RIM :])
        own_ref[at + 2 * RIM : at + 3 * RIM, :] = jnp.where(low, middle[RIM : 2 * RIM], 0.0)
    terms_ref[:, :lanes] = body_ref[...]
    clear_rims(tall, shift_ref)
    newer, older = odd_ref, even_ref
    for k in range(1, orders):
        def keep(q, fresh):
            r = q - halo
            if 0 <= r < rows:
                columns = slice(k * lanes, (k + 1) * lanes)
                first = jnp.where(low, 0.0, fresh[RIM : 2 * RIM])
                last = jnp.where(low, fresh[half : half + RIM], 0.0)
                kept = jnp.concatenate([first, fresh[2 * RIM : half], last], axis=0)
                terms_ref[r * half : (r + 1) * half, columns] = kept.astype(BF16)

        next_term(k, tall, scale_ref, newer, older, shift_ref, keep)
        newer, older = older, newer
        if k % 2:
            pair = slice((k - 1) * lanes, (k + 1) * lanes)
            sums_ref[k // 2] = order_products(lanes, feature_ref[...], terms_ref[:, pair])


def store_sums(message_ref, blocks, exponent):
    scale, at = jnp.exp2(9.0 - exponent), 0
    for block in blocks:
        for row in range(0, block.shape[0], 8):
            message_ref[at : at + 8, :] = block[row : row + 8] * scale
            at += 8
    message_ref[at:, :] = jnp.concatenate([exponent] * (NOTES // 8), axis=0)


def decoded_sums(mine_ref, received_ref):
    notes = mine_ref.shape[0] - NOTES
    mine, received = mine_ref[notes : notes + 8, :], received_ref[notes : notes + 8, :]
    scales = jnp.exp2(mine - 9.0), jnp.exp2(received - 9.0)
    sums = []
    for row in range(0, notes, 8):
        at = slice(row, row + 8)
        sums.append(mine_ref[at, :] * scales[0] + received_ref[at, :] * scales[1])
    return sums, jnp.maximum(mine, received) + 1.0


def add_kernel(mine_ref, received_ref, out_ref):
    store_sums(out_ref, *decoded_sums(mine_ref, received_ref))


def edge_kernel(
    orders, own_ref, centre_ref, second_ref, first_ref, rim_ref, sums_ref,
    terms_ref, message_ref, even_ref, odd_ref, scale_ref, wide_ref, shift_ref,
):
    rows, cols = centre_ref.shape[0] // 3, centre_ref.shape[1]
    halo, lanes, quarter = orders - 1, own_ref.shape[1], cols // 4
    channels, total, tall = lanes // 2, rows + 2 * halo, 3 * RIM
    west, east = in_order("col", first_ref[...].astype(F32), second_ref[...].astype(F32))
    lane = iota((3 * rows, cols), 1)
    masks = jnp.where(lane < quarter, west[: 3 * rows], jnp.where(lane < 3 * quarter, centre_ref[...], east[: 3 * rows]))
    across = compact_scales(masks)
    begin = quarter - RIM
    spread_scales(across[begin : begin + tall], across[3 * quarter - 2 * RIM : 3 * quarter + RIM], scale_ref)

    low = iota((RIM, lanes), 1) < channels
    for q in range(total):
        n, upper_row = q % (total // 2), q >= total // 2
        strip = slice(3 * rows + n * RIM, 3 * rows + (n + 1) * RIM)
        before = swap_halves(west[strip]) if upper_row else west[strip]
        after = east[strip] if upper_row else swap_halves(east[strip])
        at = q * tall
        odd_ref[at : at + RIM, :] = jnp.where(low, before, own_ref[at : at + RIM, :])
        odd_ref[at + RIM : at + 2 * RIM, :] = own_ref[at + RIM : at + 2 * RIM, :]
        odd_ref[at + 2 * RIM : at + tall, :] = jnp.where(low, own_ref[at + 2 * RIM : at + tall, :], after)

    wide_ref[:, :lanes] = jnp.zeros((rows * RIM, lanes), F32)
    blocks = []
    clear_rims(tall, shift_ref)
    newer, older = odd_ref, even_ref
    for k in range(1, orders):
        def keep(q, fresh):
            r = q - halo
            if 0 <= r < rows:
                wide_ref[r * RIM : (r + 1) * RIM, k * lanes : (k + 1) * lanes] = fresh[RIM : 2 * RIM]

        next_term(k, tall, scale_ref, newer, older, shift_ref, keep)
        newer, older = older, newer
        if k % 2:
            pair = slice((k - 1) * lanes, (k + 1) * lanes)
            terms = wide_ref[:, pair].astype(BF16)
            terms_ref[:, pair] = terms
            blocks.append(sums_ref[k // 2] + order_products(lanes, rim_ref[...], terms))
    tiles = [jnp.abs(block[row : row + 8]) for block in blocks for row in range(0, channels, 8)]
    largest = functools.reduce(jnp.maximum, tiles)
    exponent = jnp.floor(jnp.log2(jnp.maximum(largest, 1e-30))) + 1.0
    store_sums(message_ref, blocks, exponent)


def mix_kernel(weight_ref, inner_ref, rim_ref, grad_ref, wide_ref, terms_ref):
    channels, rows, cols = grad_ref.shape
    half, lanes = cols // 2, 2 * channels
    terms_ref[...] = inner_ref[...]
    lane, sublane = iota((2 * RIM, lanes), 1), iota((2 * RIM, lanes), 0)
    first_columns = jnp.logical_and(lane < channels, sublane < RIM)
    last_columns = jnp.logical_and(lane >= channels, sublane >= RIM)
    for k in range(1, rim_ref.shape[1] // lanes):
        columns = slice(k * lanes, (k + 1) * lanes)
        rims = rim_ref[:, columns].astype(F32)
        for r in range(rows):
            twice = jnp.concatenate([rims[r * RIM : (r + 1) * RIM]] * 2, axis=0)
            for begin, chosen in ((r * half, first_columns), ((r + 1) * half - 2 * RIM, last_columns)):
                at = (slice(begin, begin + 2 * RIM), columns)
                terms_ref[at] = jnp.where(chosen, twice, inner_ref[at].astype(F32)).astype(BF16)
    low = iota((channels, cols), 1) < half
    mixed = lax.dot_general(weight_ref[...], terms_ref[...], NT, preferred_element_type=F32)
    for q in range(rows // 2):
        upper, lower = mixed[:channels, q * cols : (q + 1) * cols], mixed[channels:, q * cols : (q + 1) * cols]
        wide_ref[pl.ds(2 * q, channels, stride=rows), :] = jnp.where(low, upper, swap_halves(lower))
        wide_ref[pl.ds(2 * q + 1, channels, stride=rows), :] = jnp.where(low, swap_halves(upper), lower)
    grad_ref[...] = wide_ref[...].reshape(channels, rows, cols).astype(BF16)


def finish_kernel(divisor, mine_ref, other_ref, out_ref):
    channels = out_ref.shape[1]
    sums, _ = decoded_sums(mine_ref, other_ref)
    for n, block in enumerate(sums):
        b, row = n * 8 // channels, n * 8 % channels
        block = block / divisor
        out_ref[2 * b, row : row + 8, :] = block[:, :channels]
        out_ref[2 * b + 1, row : row + 8, :] = block[:, channels:]


def call(kernel, outs, scratch, cost, *args):
    return pl.pallas_call(
        kernel,
        out_shape=outs,
        in_specs=[pl.BlockSpec(memory_space=pltpu.VMEM)] * len(args),
        out_specs=jax.tree.map(lambda _: pl.BlockSpec(memory_space=pltpu.VMEM), outs),
        scratch_shapes=scratch,
        compiler_params=pltpu.CompilerParams(vmem_limit_bytes=32 * 1024 * 1024),
        cost_estimate=pl.CostEstimate(flops=cost, bytes_accessed=1 << 20, transcendentals=0),
    )(*args)


def swap(x, partner):
    places = range(lax.axis_size("row") * lax.axis_size("col"))
    return lax.ppermute(x, ("row", "col"), [(i, partner(i)) for i in places])


def exchange_cols(first, second):
    across = lax.axis_size("col")

    def after_odd(i):
        row, col = i // across, i % across
        return row * across + (((col - 1) % across ^ 1) + 1) % across

    second = swap(second, after_odd)
    return swap(first, lambda i: i ^ 1), second


def exchange_rows(first, second):
    across, down = lax.axis_size("col"), lax.axis_size("row")

    def after_odd(i):
        row, col = i // across, i % across
        return i ^ 1 if row in (0, down - 1) else (((row - 1) ^ 1) + 1) * across + col

    return swap(first, lambda i: (i // across ^ 1) * across + i % across), swap(second, after_odd)


def sum_everywhere(part, work, *args):
    across, down = lax.axis_size("col"), lax.axis_size("row")
    beside = list(range(1, across.bit_length() - 1))
    below = list(range(across.bit_length() - 1, (across * down).bit_length() - 1))
    turns = [(beside[n : n + 1], below[n : n + 1]) for n in range(max(len(beside), len(below)))]
    even = [bit for a, b in turns for bit in a + b]
    odd = [bit for a, b in zip(beside[::-1] + [None] * len(below), below) for bit in ([b] if a is None else [b, a])]
    odd += [bit for bit in beside if bit not in odd]
    for n, bits in enumerate(zip(even, odd)):
        message = lax.optimization_barrier(part.astype(jnp.float16))
        received = swap(message, lambda i: i ^ (1 << bits[i.bit_count() % 2]) ^ 1)
        if n == 0:
            _, *args = lax.optimization_barrier((message, *args))
            received, done = lax.optimization_barrier((received, work(*args)))
        part = call(
            add_kernel, jax.ShapeDtypeStruct(part.shape, F32), [], 1 << 16, message.astype(F32), received.astype(F32)
        )
    message = lax.optimization_barrier(part.astype(jnp.float16))
    return message.astype(F32), swap(message, lambda i: i ^ 1).astype(F32), done


def body(feature, cotangent, order_weight, pixel_mask):
    orders, channels, _ = order_weight.shape
    _, rows, cols = feature.shape
    half, lanes, halo = cols // 2, 2 * channels, orders - 1
    tall, total = half + 2 * RIM, rows + 2 * halo
    shape = jax.ShapeDtypeStruct
    wide = pltpu.VMEM((channels * rows, cols), F32)
    marks = shape((2 * rows, cols), BF16)

    mask16 = call(mask_kernel, marks, [], 1 << 31, pixel_mask)
    sent = shape((halo * half + 2 * rows, lanes), BF16)
    cot_body, first, second = call(
        functools.partial(pack_kernel, halo), [shape((rows * half, lanes), BF16), sent, sent], [wide], 1 << 20,
        cotangent, mask16,
    )
    first, second = exchange_rows(first, second)
    features, rims, weights = call(
        early_kernel,
        [shape((lanes, rows * half), BF16), shape((lanes, rows * RIM), BF16), shape((lanes, orders * lanes), BF16)],
        [wide], 1 << 20, feature, order_weight,
    )
    sent = shape((-(-(3 * rows + total // 2 * RIM) // 16) * 16, lanes), BF16)
    west_first, west_second = call(
        functools.partial(strips_kernel, halo), [sent, sent], [], 1 << 16, cot_body, mask16, second, first
    )
    west_first, west_second = exchange_cols(west_first, west_second)
    buffer = pltpu.VMEM((total * tall, lanes), F32)
    small = pltpu.VMEM((total * 3 * RIM, lanes), F32)
    terms = shape((rows * half, orders * lanes), BF16)
    rim_terms = shape((rows * RIM, orders * lanes), BF16)
    inner, sums, own, centre = call(
        functools.partial(interior_kernel, orders),
        [
            terms, shape((orders // 2, channels, lanes), F32), shape((total * 3 * RIM, lanes), F32),
            shape((3 * rows, cols), F32),
        ],
        [buffer, buffer, buffer, pltpu.VMEM((total * (tall + 2 * RIM), lanes), F32)], 1 << 28, cot_body, mask16, second, first, features,
    )
    outer, message = call(
        functools.partial(edge_kernel, orders), [rim_terms, shape((orders // 2 * channels + NOTES, lanes), F32)],
        [small, small, small, pltpu.VMEM(rim_terms.shape, F32), pltpu.VMEM((total * 5 * RIM, lanes), F32)], 1 << 26,
        own, centre, west_second, west_first, rims, sums,
    )
    mix = functools.partial(
        call, mix_kernel, shape((channels, rows, cols), BF16), [wide, pltpu.VMEM(terms.shape, BF16)], 1 << 20
    )
    mine, other, grad_feature = sum_everywhere(message, mix, weights, inner, outer)
    pixel_count = rows * cols * lax.axis_size("row") * lax.axis_size("col")
    grad_order = call(
        functools.partial(finish_kernel, math.sqrt(pixel_count)),
        shape((orders, channels, channels), F32), [], 1 << 16, mine, other,
    )
    return (grad_feature, grad_order)


def solution(mesh):
    placed = (P(None, "row", "col"), P(None, "row", "col"), P(), P("row", "col"))
    return jax.shard_map(
        body, mesh=mesh, in_specs=placed, out_specs=(P(None, "row", "col"), P()), check_vma=False
    )
```
